512 devices in a mesh: tm: 16 (over y, x_hi), space: 32 (over z, x_lo, core).
Axes of the slice: x: 4 (x_hi: 2, x_lo: 2; x = x_hi * 2 + x_lo), y: 8, z: 8, core: 2. Of those that a mesh axis runs over, the one named last changes fastest.
Arguments:
- start_states: float32 [16, 3, 512, 2048], P('tm', None, 'space'), may hold values from -4 to 4
- lift_weight: float32 [256, 3], replicated, may hold values from -6 to 6
- lift_bias: float32 [256], replicated, may hold values from -3 to 3
- conv_weight: bfloat16 [3, 3, 256, 256], replicated, may hold values from -0.125 to 0.125
- conv_bias: float32 [256], replicated, may hold values from -3 to 3
- out_weight: bfloat16 [3, 256], replicated, may hold values from -0.1875 to 0.1875
Outputs:
- corrected: float32 [16, 3, 512, 2048], P('tm', None, 'space')
The draws below stay inside these ranges and needn't reach their ends.
All inputs are finite; a program needn't handle non-finite values.
Results may differ from the reference program's by a relative error of at most 0.017.
Values sent between devices are 32-bit elements; how exact they have to be, the bound alone decides.
No kernel may reach another device: no remote copies, remote signals or barrier semaphores. Data moves between devices by JAX's collectives and lax.ppermute only.
A program may use at most 64 MiB of HBM per device.

```python
import jax
import jax.numpy as jnp

C = 256
FINE = 4
RF = 8
NX = 2048
SLICES = 16
NY = 512


def shard_levels(stream_key, shape, shards, smallest, top_value):
    loudness, own = 1.0, jax.random.fold_in(stream_key, 6)
    for position, blocks in shards:
        steps = jnp.exp(jax.random.uniform(jax.random.fold_in(own, position), (blocks,), jnp.float32, smallest / len(shards), top_value / len(shards)))
        loudness = loudness * jnp.repeat(steps, shape[position] // blocks).reshape([-1 if axis == position else 1 for axis in range(len(shape))])
    return loudness


def gaussian(key, dims, deviation, reach, split=(), dtype=jnp.bfloat16):
    entries = jax.random.normal(key, dims, jnp.float32) * deviation
    if len(split) > 0:
        entries = shard_levels(key, dims, split, -0.22, 0.18) * entries
    return jnp.clip(entries, min=-reach, max=reach).astype(dtype)


def setup_inputs(seed: int = 0) -> dict:
    key_of = jax.random.split(jax.random.key(seed), 7)
    return {
        "start_states": gaussian(key_of[0], (SLICES, 3, NY, NX), 1.0, 4.0, ((0, 16), (2, 32)), jnp.float32),
        "lift_weight": gaussian(key_of[1], (C, 3), 1.0, 6.0, (), jnp.float32),
        "lift_bias": gaussian(key_of[2], (C,), 0.5, 3.0, (), jnp.float32),
        "conv_weight": gaussian(key_of[3], (3, 3, C, C), (9 * C) ** -0.5, 0.125),
        "conv_bias": gaussian(key_of[4], (C,), 0.5, 3.0, (), jnp.float32),
        "out_weight": gaussian(key_of[5], (3, C), (4 * C) ** -0.5, 0.1875),
    }


time_step = 0.2
viscosity = 1.0
sound_sq = 1.0


def fine_step(extended):
    center = extended[:, 1:-1, :]
    north = extended[:, :-2, :]
    south = extended[:, 2:, :]
    east = jnp.roll(center, -1, axis=2)
    west = jnp.roll(center, 1, axis=2)
    along_x = (east - west) * 0.5
    along_y = (south - north) * 0.5
    laplace = east + west + north + south - 4.0 * center
    speed_x = center[0]
    speed_y = center[1]
    new_x = speed_x + time_step * (-(speed_x * along_x[0] + speed_y * along_y[0]) - along_x[2] + viscosity * laplace[0])
    new_y = speed_y + time_step * (-(speed_x * along_x[1] + speed_y * along_y[1]) - along_y[2] + viscosity * laplace[1])
    new_p = center[2] - time_step * sound_sq * (along_x[0] + along_y[1]) + time_step * viscosity * laplace[2]
    return jnp.stack([new_x, new_y, new_p])


def periodic_rows(state_slab, width):
    return jnp.concatenate([state_slab[:, -width:, :], state_slab, state_slab[:, :width, :]], axis=1)


def restrict(state_slab):
    fields, rows, columns = state_slab.shape
    return state_slab.reshape(fields, rows // RF, RF, columns // RF, RF).mean(axis=(2, 4))


def prolong(coarse):
    return jnp.repeat(jnp.repeat(coarse, RF, axis=1), RF, axis=2)


def apply_net(extended, lift_weight, lift_bias, conv_weight, conv_bias, out_weight):
    rows = extended.shape[1] - 2
    columns = extended.shape[2]
    channels = conv_weight.shape[2]
    lifted = lift_bias[:, None, None] + lift_weight[:, 0, None, None] * extended[0]
    lifted = lifted + lift_weight[:, 1, None, None] * extended[1] + lift_weight[:, 2, None, None] * extended[2]
    hidden = jax.nn.gelu(lifted).astype(jnp.bfloat16)
    accumulated = jnp.zeros((channels, rows * columns), jnp.float32)
    for row_tap in range(3):
        for col_tap in range(3):
            shifted = jnp.roll(hidden[:, row_tap:row_tap + rows, :], 1 - col_tap, axis=2)
            accumulated = accumulated + jnp.dot(conv_weight[row_tap, col_tap], shifted.reshape(channels, rows * columns), preferred_element_type=jnp.float32)
    activated = jax.nn.gelu(accumulated + conv_bias[:, None]).astype(jnp.bfloat16)
    increment = jnp.dot(out_weight, activated, preferred_element_type=jnp.float32)
    return extended[:, 1:-1, :] + increment.reshape(3, rows, columns)


def reference(start_states, lift_weight, lift_bias, conv_weight, conv_bias, out_weight):
    weights = (lift_weight, lift_bias, conv_weight, conv_bias, out_weight)
    corrections = []
    for slice_number in range(SLICES):
        state_slab = start_states[slice_number]
        fine_end = state_slab
        for repeat in range(FINE):
            fine_end = fine_step(periodic_rows(fine_end, 1))
        guess = apply_net(periodic_rows(restrict(state_slab), 1), *weights)
        corrections.append(fine_end - prolong(guess))
    coarse = restrict(start_states[0])
    results = []
    for slice_number in range(SLICES):
        advanced = apply_net(periodic_rows(coarse, 1), *weights)
        results.append(prolong(advanced) + corrections[slice_number])
        coarse = advanced + restrict(corrections[slice_number])
    return jnp.stack(results)
```

```python
import functools
import jax, jax.numpy as jnp
from jax import lax
from jax.experimental import pallas as pl
from jax.experimental.pallas import tpu as pltpu
from jax.sharding import PartitionSpec as P

f32, bf16 = jnp.float32, jnp.bfloat16
FINE = 4
RF = 8
time_step = 0.2
viscosity = 1.0
sound_sq = 1.0
N = 16
ROWS = 32
W1, W2 = 48, 32

def gelu(x):
    u = x * (0.7978845608028654 + 0.035677408136300125 * (x * x))
    h = 0.5 * x
    return h + h * jnp.tanh(u)

def lift_operand(s, lane):
    hi = s.astype(bf16)
    lo = (s - hi.astype(f32)).astype(bf16)
    one = jnp.ones_like(hi)
    return jnp.concatenate([jnp.where(lane < 64, hi, lo), jnp.where(lane < 64, hi, one)], axis=1)

def shifted(h, axis_size):
    return pltpu.roll(h, 1, 0), pltpu.roll(h, axis_size - 1, 0)

def chain_kernel(CR_L, CR_C, r_ref, wt_ref, lw_ref, ow_ref, cb_ref, out_ref, d_ref, s_ref, h_ref, lwm_ref, owm_ref):
    acc = r_ref[0]
    d_ref[0:4] = jnp.zeros((4, ROWS * W1), f32)
    d_ref[4:8] = acc
    for n in range(1, N - 1):
        acc = acc + r_ref[n]
        d_ref[4 * n + 4:4 * n + 8] = acc
    for q in range(ROWS * W1 // 128):
        t = d_ref[:, q * 128:(q + 1) * 128].T
        s_ref[q * 128:(q + 1) * 128, :] = jnp.concatenate([t, t], axis=1)
    krow = lax.broadcasted_iota(jnp.int32, (256, 256), 0)
    kslot = (krow & 63) >> 2
    ocol = (lax.broadcasted_iota(jnp.int32, (256, 128), 1) & 63) >> 2

    def step(m, k, pitch):
        off = (W1 - pitch) // 2
        lwm_ref[...] = jnp.where((kslot == m) | (krow >= 192), lw_ref[...].astype(f32), 0.0).astype(bf16)
        owm_ref[...] = jnp.where(ocol >= m, ow_ref[...].astype(f32), 0.0).astype(bf16)
        r_lo, r_hi = 14 - k, 18 + k

        def lift(row, n):
            cells = n * pitch
            if pitch == W1:
                s = s_ref[pl.ds(pl.multiple_of(row * W1, 16), cells), :]
            else:
                s = jnp.concatenate([s_ref[pl.ds(pl.multiple_of((row + i) * W1 + off, 8), pitch), :] for i in range(n)], axis=0)
            lane = lax.broadcasted_iota(jnp.int32, s.shape, 1)
            x = lift_operand(s, lane)
            h = gelu(jnp.dot(x, lwm_ref[...], preferred_element_type=f32))
            left, right = shifted(h, cells)
            dst = pl.ds(pl.multiple_of(row * pitch, 16), cells)
            h_ref[dst, 0:256] = left.astype(bf16)
            h_ref[dst, 256:512] = h.astype(bf16)
            h_ref[dst, 512:768] = right.astype(bf16)

        def conv(row, n):
            cells = n * pitch
            acc = None
            for di in range(3):
                src = pl.ds(pl.multiple_of((row + di - 1) * pitch, 16), cells)
                p = jnp.dot(h_ref[src, :], wt_ref[di], preferred_element_type=f32)
                acc = p if acc is None else acc + p
            act = gelu(acc + cb_ref[...]).astype(bf16)
            inc = jnp.dot(act, owm_ref[...], preferred_element_type=f32)
            if pitch == W1:
                dst = pl.ds(pl.multiple_of(row * W1, 16), cells)
                s_ref[dst, :] = s_ref[dst, :] + inc
            else:
                for i in range(n):
                    dst = pl.ds(pl.multiple_of((row + i) * W1 + off, 8), pitch)
                    s_ref[dst, :] = s_ref[dst, :] + inc[i * pitch:(i + 1) * pitch]

        def sweep(body, lo, hi, chunk):
            full = (hi - lo) // chunk
            if full > 1:
                lax.fori_loop(0, full, lambda i, c: (body(lo + i * chunk, chunk), c)[1], 0)
            elif full == 1:
                body(lo, chunk)
            rest = (hi - lo) % chunk
            if rest:
                body(lo + full * chunk, rest)

        sweep(lift, r_lo, r_hi, CR_L)
        sweep(conv, r_lo + 1, r_hi - 1, CR_C)

    for m in range(1, N):
        k = N - 1 - m
        step(m, k, W1 if k > 7 else W2)
    g = jnp.concatenate([s_ref[15 * W1 + 16:15 * W1 + 32, :], s_ref[16 * W1 + 16:16 * W1 + 32, :]], axis=0)
    gt = g.T
    for n in range(N):
        out_ref[n] = gt[4 * n:4 * n + 4, :]

def chain(recv, wt, lw, ow, cb, CR_L=8, CR_C=8):
    L = ROWS * W1
    vm = pl.BlockSpec(memory_space=pltpu.VMEM)
    return pl.pallas_call(
        functools.partial(chain_kernel, CR_L, CR_C),
        out_shape=jax.ShapeDtypeStruct((N, 4, 32), f32),
        in_specs=[vm] * 5, out_specs=vm,
        scratch_shapes=[pltpu.VMEM((64, L), f32), pltpu.VMEM((L, 128), f32), pltpu.VMEM((L, 768), bf16),
                        pltpu.VMEM((256, 256), bf16), pltpu.VMEM((256, 128), bf16)],
        compiler_params=pltpu.CompilerParams(vmem_limit_bytes=48 * 2**20),
    )(recv, wt, lw, ow, cb)

def tables(lift_weight, lift_bias, conv_weight, conv_bias, out_weight):
    wt = conv_weight.transpose(0, 1, 3, 2).reshape(3, 768, 256)
    w4 = jnp.concatenate([lift_weight.T, jnp.zeros((1, 256), f32)], 0)
    hi = w4.astype(bf16); lo = (w4 - hi.astype(f32)).astype(bf16)
    bh = lift_bias.astype(bf16); bl = (lift_bias - bh.astype(f32)).astype(bf16)
    lw = jnp.concatenate([jnp.tile(hi, (32, 1)), jnp.tile(lo, (16, 1)), bh[None], bl[None], jnp.zeros((62, 256), bf16)], 0)
    ow = jnp.tile(jnp.concatenate([out_weight, jnp.zeros((1, 256), bf16)], 0), (32, 1)).T
    return wt, lw, ow, conv_bias[None]

def thirds(x):
    hi = x.astype(bf16)
    rest = x - hi.astype(f32)
    mid = rest.astype(bf16)
    low = (rest - mid.astype(f32)).astype(bf16)
    return jnp.concatenate([hi, mid, low], axis=0)

def exact_dot(x, pattern):
    n = x.shape[0]
    y = jnp.dot(thirds(x), pattern, preferred_element_type=f32)
    return y[0:n] + y[n:2 * n] + y[2 * n:3 * n]

def fine_step(a, b, q):
    def parts(x):
        e, w = pltpu.roll(x, x.shape[1] - 1, 1), pltpu.roll(x, 1, 1)
        n, s = pltpu.roll(x, 1, 0), pltpu.roll(x, x.shape[0] - 1, 0)
        return e - w, s - n, (e + w) + (n + s)
    ax, ay, al = parts(a)
    bx, by, bl = parts(b)
    qx, qy, ql = parts(q)
    half, keep = 0.5 * time_step, 1.0 - 4.0 * time_step * viscosity
    new_a = keep * a + time_step * viscosity * al - half * (a * ax + b * ay + qx)
    new_b = keep * b + time_step * viscosity * bl - half * (a * bx + b * by + qy)
    new_q = keep * q + time_step * viscosity * ql - half * sound_sq * (ax + by)
    return new_a, new_b, new_q

def first_kernel(tm_ref, s_ref, up_ref, dn_ref, wt_ref, lw_ref, ow_ref, cb_ref, corr_ref, c_ref, q_ref, h_ref):
    fields = [jnp.concatenate([up_ref[f], s_ref[0, f], dn_ref[f]], axis=0) for f in range(3)]
    q_ref[...] = jnp.zeros(q_ref.shape, f32)
    for f in range(3):
        for r in range(4):
            q_ref[4 * r + f:4 * r + f + 1, :] = jnp.sum(fields[f][8 * r:8 * r + 8], axis=0, keepdims=True)
    for _ in range(FINE):
        fields = fine_step(*fields)
    for f in range(3):
        for r in range(2):
            q_ref[16 + 4 * r + f:17 + 4 * r + f, :] = jnp.sum(fields[f][8 + 8 * r:16 + 8 * r], axis=0, keepdims=True)
    half = 128 * RF
    pool = (lax.broadcasted_iota(jnp.int32, (half, 128), 0) // RF == lax.broadcasted_iota(jnp.int32, (half, 128), 1)).astype(f32).astype(bf16)
    spread = (lax.broadcasted_iota(jnp.int32, (128, half), 1) // RF == lax.broadcasted_iota(jnp.int32, (128, half), 0)).astype(f32).astype(bf16)
    pooled = jnp.concatenate([exact_dot(q_ref[:, 0:half], pool), exact_dot(q_ref[:, half:], pool)], axis=1) * (1.0 / (RF * RF))
    pad = jnp.zeros((48, 256), f32)
    s = jnp.concatenate([pooled[0:16], pad, pooled[0:16], pad], axis=0).T
    x = lift_operand(s, lax.broadcasted_iota(jnp.int32, s.shape, 1))
    krow = lax.broadcasted_iota(jnp.int32, (256, 256), 0)
    kslot = (krow & 63) >> 2
    lw = lw_ref[...].astype(f32)
    for r in range(4):
        lwm = jnp.where((kslot == r) | (krow >= 192), lw, 0.0).astype(bf16)
        h = gelu(jnp.dot(x, lwm, preferred_element_type=f32))
        left, right = shifted(h, 256)
        h_ref[256 * r:256 * r + 256, 0:256] = left.astype(bf16)
        h_ref[256 * r:256 * r + 256, 256:512] = h.astype(bf16)
        h_ref[256 * r:256 * r + 256, 512:768] = right.astype(bf16)
    acc = jnp.dot(h_ref[0:512], wt_ref[0], preferred_element_type=f32)
    acc = acc + jnp.dot(h_ref[256:768], wt_ref[1], preferred_element_type=f32)
    acc = acc + jnp.dot(h_ref[512:1024], wt_ref[2], preferred_element_type=f32)
    act = gelu(acc + cb_ref[...]).astype(bf16)
    inc = jnp.dot(act, ow_ref[...], preferred_element_type=f32)
    lane = lax.broadcasted_iota(jnp.int32, s.shape, 1)
    guess = (s + jnp.where(lane < 8, inc[0:256], inc[256:512])).T[4:12]
    first = jnp.where(tm_ref[0] == 0, guess, 0.0)
    c = first + (pooled[16:24] - guess)
    for i in range(c_ref.shape[0]):
        c_ref[i] = c
    delta = guess - first
    for p in range(2):
        wide = exact_dot(delta[:, 128 * p:128 * p + 128], spread)
        for f in range(3):
            for r in range(2):
                corr_ref[f, 8 * r:8 * r + 8, half * p:half * p + half] = fields[f][8 + 8 * r:16 + 8 * r, half * p:half * p + half] - wide[4 * r + f:4 * r + f + 1]

def window_kernel(sp_ref, b_ref, out_ref):
    count = b_ref.shape[0]
    for q in range(ROWS):
        dev = lax.rem(sp_ref[0] + (count - 8 + (q + 1) // 2), count)
        r = (q + 1) % 2
        v = b_ref[dev, 4 * r:4 * r + 4, :]
        ext = jnp.concatenate([v[:, 240:256], v, v[:, 0:16]], axis=1)
        for j in range(N):
            out_ref[j, :, q * W1:(q + 1) * W1] = ext[:, 16 * j:16 * j + W1]

def last_kernel(g_ref, corr_ref, out_ref, y_ref):
    for j in range(N):
        y_ref[4 * j:4 * j + 4, :] = g_ref[j]
    row = lax.broadcasted_iota(jnp.int32, (32, 128), 0)
    col = lax.broadcasted_iota(jnp.int32, (32, 128), 1)
    for r in range(2):
        pattern = (row - 16 * r == col // RF).astype(f32).astype(bf16)
        y = exact_dot(y_ref[...], pattern)
        for j in range(N):
            for f in range(3):
                out_ref[0, f, 8 * r:8 * r + 8, 128 * j:128 * j + 128] = corr_ref[f, 8 * r:8 * r + 8, 128 * j:128 * j + 128] + y[4 * j + f:4 * j + f + 1]

def shards(start_states, lift_weight, lift_bias, conv_weight, conv_bias, out_weight):
    vm = pl.BlockSpec(memory_space=pltpu.VMEM)
    sm = pl.BlockSpec(memory_space=pltpu.SMEM)
    params = pltpu.CompilerParams(vmem_limit_bytes=48 * 2**20)
    count = lax.axis_size("space")
    slab = start_states[0]
    up = lax.ppermute(slab[:, 8:], "space", [(i, (i + 1) % count) for i in range(count)])
    down = lax.ppermute(slab[:, :8], "space", [((i + 1) % count, i) for i in range(count)])
    weights = tables(lift_weight, lift_bias, conv_weight, conv_bias, out_weight)
    tm = lax.axis_index("tm").astype(jnp.int32).reshape(1)
    sp = lax.axis_index("space").astype(jnp.int32).reshape(1)
    corr, c = pl.pallas_call(
        first_kernel,
        out_shape=[jax.ShapeDtypeStruct(slab.shape, f32), jax.ShapeDtypeStruct((count, 8, 256), f32)],
        in_specs=[sm] + [vm] * 7, out_specs=[vm, vm],
        scratch_shapes=[pltpu.VMEM((24, slab.shape[2]), f32), pltpu.VMEM((1024, 768), bf16)],
        compiler_params=params, name="fine_and_guess",
    )(tm, start_states, up, down, *weights)
    c = lax.all_to_all(c, "space", 0, 0)
    send = pl.pallas_call(
        window_kernel, out_shape=jax.ShapeDtypeStruct((N, 4, ROWS * W1), f32),
        in_specs=[sm, vm], out_specs=vm, compiler_params=params, name="windows",
    )(sp, c)
    recv = lax.all_to_all(send, "tm", 0, 0)
    g = chain(recv, *weights)
    g = lax.all_to_all(g, "tm", 0, 0)
    return pl.pallas_call(
        last_kernel, out_shape=jax.ShapeDtypeStruct(start_states.shape, f32),
        in_specs=[vm, vm], out_specs=vm, scratch_shapes=[pltpu.VMEM((64, 32), f32)],
        compiler_params=params, name="correct",
    )(g, corr)

def solution(mesh):
    return jax.shard_map(
        shards, mesh=mesh,
        in_specs=(P("tm", None, "space", None), P(), P(), P(), P(), P()),
        out_specs=P("tm", None, "space", None), check_vma=False,
    )
```

```python
import functools
import jax, jax.numpy as jnp
from jax import lax
from jax.experimental import pallas as pl
from jax.experimental.pallas import tpu as pltpu
from jax.sharding import PartitionSpec as P

f32, bf16 = jnp.float32, jnp.bfloat16
FINE = 4
RF = 8
time_step = 0.2
viscosity = 1.0
sound_sq = 1.0
N = 16
ROWS = 32
W1, W2 = 48, 32

def twice_gelu(x):
    u = x * (0.7978845608028654 + 0.035677408136300125 * (x * x))
    return x + x * jnp.tanh(u)

def lift_operand(s, lane):
    hi = s.astype(bf16)
    lo = (s - hi.astype(f32)).astype(bf16)
    one = jnp.ones_like(hi)
    return jnp.concatenate([jnp.where(lane < 64, hi, lo), jnp.where(lane < 64, hi, one)], axis=1)

def shifted(h, axis_size):
    return pltpu.roll(h, 1, 0), pltpu.roll(h, axis_size - 1, 0)

def chain_kernel(SPLITS, r_ref, wt_ref, lw_ref, ow_ref, cb_ref, out_ref, d_ref, s_ref, top_ref, low_ref, *h_refs):
    part = ROWS * W1 // 4
    acc = r_ref[0]
    d_ref[0:4] = jnp.zeros((4, 3 * part), f32)
    d_ref[4:8] = acc
    for n in range(1, N - 1):
        acc = acc + r_ref[n]
        d_ref[4 * n + 4:4 * n + 8] = acc
    field = lax.broadcasted_iota(jnp.int32, (128, 128), 1) & 3
    for t in range(part // 128):
        turned = [d_ref[:, f * part + t * 128:f * part + t * 128 + 128].T for f in range(3)]
        turned = [jnp.concatenate([x, x], axis=1) for x in turned]
        for u in range(4):
            s = jnp.zeros((128, 128), f32)
            for f in range(3):
                moved = turned[f] if f == u else pltpu.roll(turned[f], (f - u) % 128, 1)
                s = jnp.where(field == f, moved, s)
            s_ref[u * part + t * 128:u * part + t * 128 + 128, :] = s
    krow = lax.broadcasted_iota(jnp.int32, (256, 256), 0)
    kslot = (krow & 63) >> 2
    ocol = (lax.broadcasted_iota(jnp.int32, (256, 128), 1) & 63) >> 2
    lw, ow = lw_ref[...].astype(f32), ow_ref[...].astype(f32)

    def rows_of(row, n, pitch):
        if pitch == W1:
            return [pl.ds(row * W1, n * W1)]
        return [pl.ds((row + i) * W1 + (W1 - pitch) // 2, pitch) for i in range(n)]

    def pitch_of(m):
        return W1 if m < 8 else W2

    def lift(m, lo, hi):
        if hi <= lo:
            return
        n, pitch, h = hi - lo, pitch_of(m), h_refs[m % 2]
        cells = n * pitch
        s = jnp.concatenate([s_ref[d, :] for d in rows_of(lo, n, pitch)], axis=0)
        lane = lax.broadcasted_iota(jnp.int32, s.shape, 1)
        lwm = jnp.where((kslot == m) | (krow >= 192), lw, 0.0).astype(bf16)
        y = twice_gelu(jnp.dot(lift_operand(s, lane), lwm, preferred_element_type=f32))
        left, right = shifted(y, cells)
        dst = pl.ds(lo * pitch, cells)
        h[dst, 0:256] = left.astype(bf16)
        h[dst, 256:512] = y.astype(bf16)
        h[dst, 512:768] = right.astype(bf16)

    def conv(m, lo, hi):
        n, pitch, h = hi - lo, pitch_of(m), h_refs[m % 2]
        x = jnp.concatenate([h[pl.ds((lo + di - 1) * pitch, n * pitch), :] for di in range(3)], axis=1)
        return jnp.dot(x, wt_ref[...].reshape(2304, 256), preferred_element_type=f32)

    def finish(m, lo, hi, acc):
        n, pitch = hi - lo, pitch_of(m)
        act = twice_gelu(acc + cb_ref[...]).astype(bf16)
        owm = jnp.where(ocol >= m, ow, 0.0).astype(bf16)
        inc = jnp.dot(act, owm, preferred_element_type=f32)
        at = 0
        for d in rows_of(lo, n, pitch):
            s_ref[d, :] = s_ref[d, :] + inc[at:at + d.size]
            at += d.size

    splits = SPLITS

    def block(body):
        body()

    def store_conv(m, lo, hi, acc_ref):
        if hi > lo:
            acc_ref[0:(hi - lo) * pitch_of(m), :] = conv(m, lo, hi)

    def finish_from(m, lo, hi, acc_ref):
        if hi > lo:
            finish(m, lo, hi, acc_ref[0:(hi - lo) * pitch_of(m), :])

    lift(1, 0, splits[1] + 1)
    done = splits[1] + 1
    for m in range(1, N + 1):
        prev = (m - 1, splits[m - 1], 33 - m)
        if m == N:
            block(lambda: finish_from(*prev, low_ref))
            break
        lo, hi, b = m, 32 - m, splits[m]
        need = min(b + 1, hi + 1)
        if done < need:
            def catch_up():
                if m > 1:
                    finish_from(*prev, low_ref)
                lift(m, done, need)
            block(catch_up)
            done, prev = need, (m - 1, 0, 0)

        def upper():
            store_conv(m, lo, min(b, hi), top_ref)
            if m > 1:
                finish_from(*prev, low_ref)
            lift(m, done, hi + 1)
        block(upper)
        early = m if m + 1 == N else max(m, min(b, splits[m + 1] + 1))

        def lower():
            store_conv(m, b, hi, low_ref)
            finish_from(m, lo, min(b, hi), top_ref)
            if m + 1 < N:
                lift(m + 1, m, early)
        block(lower)
        done = early
    g = jnp.concatenate([s_ref[15 * W1 + 16:15 * W1 + 32, :], s_ref[16 * W1 + 16:16 * W1 + 32, :]], axis=0)
    gt = g.T
    for n in range(N):
        for f in range(3):
            out_ref[n, :, 32 * f:32 * f + 32] = gt[4 * n + f:4 * n + f + 1, :]
        out_ref[n, :, 96:128] = jnp.zeros((1, 32), f32)

SPLITS = (0, 19, 18, 17, 16, 15, 14, 13, 17, 16, 15, 14, 20, 19, 18, 17)

def chain(recv, wt, lw, ow, cb, SPLITS=SPLITS):
    L = ROWS * W1
    vm = pl.BlockSpec(memory_space=pltpu.VMEM)
    return pl.pallas_call(
        functools.partial(chain_kernel, tuple(SPLITS)),
        out_shape=jax.ShapeDtypeStruct((N, 1, 128), f32),
        in_specs=[vm] * 5, out_specs=vm,
        scratch_shapes=[pltpu.VMEM((64, 3 * L // 4), f32), pltpu.VMEM((L, 128), f32), pltpu.VMEM((L, 256), f32), pltpu.VMEM((L, 256), f32),
                        pltpu.VMEM((L, 768), bf16), pltpu.VMEM((L, 768), bf16)],
        compiler_params=pltpu.CompilerParams(vmem_limit_bytes=48 * 2**20),
    )(recv, wt, lw, ow, cb)

def table_kernel(lwt_ref, lb_ref, cw_ref, ow_ref, wt_ref, lw_ref, owr_ref, wide_ref, rows_ref):
    for i in range(3):
        for j in range(3):
            wt_ref[i, 256 * j:256 * j + 256, :] = (0.5 * cw_ref[i, j].astype(f32)).T.astype(bf16)
    wide_ref[...] = jnp.zeros(wide_ref.shape, f32)
    wide_ref[:, 0:3] = lwt_ref[...]
    w = wide_ref[...].T[0:8]
    hi = w.astype(bf16).astype(f32)
    rows_ref[0:8, :] = hi
    rows_ref[8:16, :] = w - hi
    b = lb_ref[...]
    bhi = b.astype(bf16).astype(f32)
    rows_ref[3:4, :] = bhi
    rows_ref[11:12, :] = b - bhi
    k = lax.broadcasted_iota(jnp.int32, (256, 16), 0)
    col = lax.broadcasted_iota(jnp.int32, (256, 16), 1)
    field = k & 3
    weight = (k < 192) & (field < 3) & (col == field + jnp.where(k < 128, 0, 8))
    bias = ((k == 192) & (col == 3)) | ((k == 193) & (col == 11))
    pick = jnp.where(weight | bias, 1.0, 0.0).astype(bf16)
    lw_ref[...] = jnp.dot(pick, rows_ref[...].astype(bf16), preferred_element_type=f32).astype(bf16)
    rows_ref[...] = jnp.zeros(rows_ref.shape, f32)
    rows_ref[0:3, :] = 0.5 * ow_ref[...].astype(f32)
    lane = lax.broadcasted_iota(jnp.int32, (128, 16), 0) & 3
    pick = jnp.where((lane < 3) & (lane == lax.broadcasted_iota(jnp.int32, (128, 16), 1)), 1.0, 0.0).astype(bf16)
    owr_ref[...] = jnp.dot(pick, rows_ref[...].astype(bf16), preferred_element_type=f32).T.astype(bf16)

def tables(lift_weight, lift_bias, conv_weight, conv_bias, out_weight):
    vm = pl.BlockSpec(memory_space=pltpu.VMEM)
    wt, lw, ow = pl.pallas_call(
        table_kernel,
        out_shape=[jax.ShapeDtypeStruct((3, 768, 256), bf16), jax.ShapeDtypeStruct((256, 256), bf16), jax.ShapeDtypeStruct((256, 128), bf16)],
        in_specs=[vm] * 4, out_specs=[vm] * 3,
        scratch_shapes=[pltpu.VMEM((256, 128), f32), pltpu.VMEM((16, 256), f32)],
        compiler_params=pltpu.CompilerParams(vmem_limit_bytes=32 * 2**20),
        cost_estimate=pl.CostEstimate(flops=10**7, bytes_accessed=10**7, transcendentals=0), name="tables",
    )(lift_weight, lift_bias[None], conv_weight, out_weight)
    return wt, lw, ow, conv_bias[None]

def thirds(x):
    hi = x.astype(bf16)
    rest = x - hi.astype(f32)
    mid = rest.astype(bf16)
    low = (rest - mid.astype(f32)).astype(bf16)
    return jnp.concatenate([hi, mid, low], axis=0)

def exact_dot(x, pattern):
    n = x.shape[0]
    y = jnp.dot(thirds(x), pattern, preferred_element_type=f32)
    return y[0:n] + y[n:2 * n] + y[2 * n:3 * n]

def fine_step(a, b, q):
    def parts(x):
        e, w = pltpu.roll(x, x.shape[1] - 1, 1), pltpu.roll(x, 1, 1)
        n, s = pltpu.roll(x, 1, 0), pltpu.roll(x, x.shape[0] - 1, 0)
        return e - w, s - n, (e + w) + (n + s)
    ax, ay, al = parts(a)
    bx, by, bl = parts(b)
    qx, qy, ql = parts(q)
    half, keep = 0.5 * time_step, 1.0 - 4.0 * time_step * viscosity
    new_a = keep * a + time_step * viscosity * al - half * (a * ax + b * ay + qx)
    new_b = keep * b + time_step * viscosity * bl - half * (a * bx + b * by + qy)
    new_q = keep * q + time_step * viscosity * ql - half * sound_sq * (ax + by)
    return new_a, new_b, new_q

def first_kernel(tm_ref, s_ref, up_ref, dn_ref, wt_ref, lw_ref, ow_ref, cb_ref, corr_ref, c_ref, q_ref, h_ref):
    fields = [jnp.concatenate([up_ref[f], s_ref[0, f], dn_ref[f]], axis=0) for f in range(3)]
    q_ref[...] = jnp.zeros(q_ref.shape, f32)
    for f in range(3):
        for r in range(4):
            q_ref[4 * r + f:4 * r + f + 1, :] = jnp.sum(fields[f][8 * r:8 * r + 8], axis=0, keepdims=True)
    for _ in range(FINE):
        fields = fine_step(*fields)
    for f in range(3):
        for r in range(2):
            q_ref[16 + 4 * r + f:17 + 4 * r + f, :] = jnp.sum(fields[f][8 + 8 * r:16 + 8 * r], axis=0, keepdims=True)
    half = 128 * RF
    pool = (lax.broadcasted_iota(jnp.int32, (half, 128), 0) // RF == lax.broadcasted_iota(jnp.int32, (half, 128), 1)).astype(f32).astype(bf16)
    spread = (lax.broadcasted_iota(jnp.int32, (128, half), 1) // RF == lax.broadcasted_iota(jnp.int32, (128, half), 0)).astype(f32).astype(bf16)
    pooled = jnp.concatenate([exact_dot(q_ref[:, 0:half], pool), exact_dot(q_ref[:, half:], pool)], axis=1) * (1.0 / (RF * RF))
    pad = jnp.zeros((48, 256), f32)
    s = jnp.concatenate([pooled[0:16], pad, pooled[0:16], pad], axis=0).T
    x = lift_operand(s, lax.broadcasted_iota(jnp.int32, s.shape, 1))
    krow = lax.broadcasted_iota(jnp.int32, (256, 256), 0)
    kslot = (krow & 63) >> 2
    lw = lw_ref[...].astype(f32)
    for r in range(4):
        lwm = jnp.where((kslot == r) | (krow >= 192), lw, 0.0).astype(bf16)
        h = twice_gelu(jnp.dot(x, lwm, preferred_element_type=f32))
        left, right = shifted(h, 256)
        h_ref[256 * r:256 * r + 256, 0:256] = left.astype(bf16)
        h_ref[256 * r:256 * r + 256, 256:512] = h.astype(bf16)
        h_ref[256 * r:256 * r + 256, 512:768] = right.astype(bf16)
    acc = jnp.dot(h_ref[0:512], wt_ref[0], preferred_element_type=f32)
    acc = acc + jnp.dot(h_ref[256:768], wt_ref[1], preferred_element_type=f32)
    acc = acc + jnp.dot(h_ref[512:1024], wt_ref[2], preferred_element_type=f32)
    act = twice_gelu(acc + cb_ref[...]).astype(bf16)
    inc = jnp.dot(act, ow_ref[...], preferred_element_type=f32)
    lane = lax.broadcasted_iota(jnp.int32, s.shape, 1)
    guess = (s + jnp.where(lane < 8, inc[0:256], inc[256:512])).T[4:12]
    first = jnp.where(tm_ref[0] == 0, guess, 0.0)
    c = first + (pooled[16:24] - guess)
    for i in range(c_ref.shape[0]):
        c_ref[i] = c
    delta = guess - first
    for p in range(2):
        wide = exact_dot(delta[:, 128 * p:128 * p + 128], spread)
        for f in range(3):
            for r in range(2):
                corr_ref[f, 8 * r:8 * r + 8, half * p:half * p + half] = fields[f][8 + 8 * r:16 + 8 * r, half * p:half * p + half] - wide[4 * r + f:4 * r + f + 1]

def window_kernel(sp_ref, b_ref, out_ref, w_ref):
    count = b_ref.shape[0]
    for q in range(ROWS):
        dev = lax.rem(sp_ref[0] + (count - 8 + (q + 1) // 2), count)
        r = (q + 1) % 2
        for f in range(3):
            w_ref[3 * (q % 8) + f, q // 8:q // 8 + 1, :] = b_ref[dev, 4 * r + f:4 * r + f + 1, :]
    for i in range(8):
        for f in range(3):
            v = w_ref[3 * i + f]
            ext = jnp.concatenate([v[:, 240:256], v, v[:, 0:16]], axis=1)
            at = f * 8 * W1 + i * W1
            for j in range(N):
                out_ref[j, :, at:at + W1] = ext[:, 16 * j:16 * j + W1]

def last_kernel(g_ref, corr_ref, out_ref, y_ref):
    for j in range(N):
        y_ref[j:j + 1, :] = g_ref[j]
    parts = thirds(y_ref[...])
    row = lax.broadcasted_iota(jnp.int32, (128, 128), 0)
    col = lax.broadcasted_iota(jnp.int32, (128, 128), 1)
    for r in range(2):
        for f in range(3):
            pattern = (row - 32 * f - 16 * r == col // RF).astype(f32).astype(bf16)
            y = jnp.dot(parts, pattern, preferred_element_type=f32)
            y = y[0:N] + y[N:2 * N] + y[2 * N:3 * N]
            for j in range(N):
                at = 128 * j
                out_ref[0, f, 8 * r:8 * r + 8, at:at + 128] = corr_ref[f, 8 * r:8 * r + 8, at:at + 128] + y[j:j + 1]

def shards(start_states, lift_weight, lift_bias, conv_weight, conv_bias, out_weight):
    vm = pl.BlockSpec(memory_space=pltpu.VMEM)
    sm = pl.BlockSpec(memory_space=pltpu.SMEM)
    params = pltpu.CompilerParams(vmem_limit_bytes=48 * 2**20)
    count = lax.axis_size("space")
    slab = start_states[0]
    up = lax.ppermute(slab[:, 8:], "space", [(i, (i + 1) % count) for i in range(count)])
    down = lax.ppermute(slab[:, :8], "space", [((i + 1) % count, i) for i in range(count)])
    weights = tables(lift_weight, lift_bias, conv_weight, conv_bias, out_weight)
    tm = lax.axis_index("tm").astype(jnp.int32).reshape(1)
    sp = lax.axis_index("space").astype(jnp.int32).reshape(1)
    corr, c = pl.pallas_call(
        first_kernel,
        out_shape=[jax.ShapeDtypeStruct(slab.shape, f32), jax.ShapeDtypeStruct((count, 8, 256), f32)],
        in_specs=[sm] + [vm] * 7, out_specs=[vm, vm],
        scratch_shapes=[pltpu.VMEM((24, slab.shape[2]), f32), pltpu.VMEM((1024, 768), bf16)],
        compiler_params=params, name="fine_and_guess",
    )(tm, start_states, up, down, *weights)
    c = lax.all_to_all(c, "space", 0, 0)
    send = pl.pallas_call(
        window_kernel, out_shape=jax.ShapeDtypeStruct((N, 4, 3 * ROWS * W1 // 4), f32),
        in_specs=[sm, vm], out_specs=vm, scratch_shapes=[pltpu.VMEM((24, 4, 256), f32)],
        compiler_params=params, name="windows",
    )(sp, c)
    recv = lax.all_to_all(send, "tm", 0, 0)
    g = chain(recv, *weights)
    g = lax.all_to_all(g, "tm", 0, 0)
    return pl.pallas_call(
        last_kernel, out_shape=jax.ShapeDtypeStruct(start_states.shape, f32),
        in_specs=[vm, vm], out_specs=vm, scratch_shapes=[pltpu.VMEM((N, 128), f32)],
        compiler_params=params, name="correct",
    )(g, corr)

def solution(mesh):
    return jax.shard_map(
        shards, mesh=mesh,
        in_specs=(P("tm", None, "space", None), P(), P(), P(), P(), P()),
        out_specs=P("tm", None, "space", None), check_vma=False,
    )
```

```python
import functools
import jax, jax.numpy as jnp
from jax import lax
from jax.experimental import pallas as pl
from jax.experimental.pallas import tpu as pltpu
from jax.sharding import PartitionSpec as P

f32, bf16 = jnp.float32, jnp.bfloat16
FINE = 4
RF = 8
time_step = 0.2
viscosity = 1.0
sound_sq = 1.0
N = 16
ROWS = 32
W1, W2 = 48, 32

def twice_gelu(x):
    u = x * (0.7978845608028654 + 0.035677408136300125 * (x * x))
    return x + x * jnp.tanh(u)

def lift_operand(s, lane):
    hi = s.astype(bf16)
    lo = (s - hi.astype(f32)).astype(bf16)
    one = jnp.ones_like(hi)
    return jnp.concatenate([jnp.where(lane < 64, hi, lo), jnp.where(lane < 64, hi, one)], axis=1)

def shifted(h, axis_size):
    return pltpu.roll(h, 1, 0), pltpu.roll(h, axis_size - 1, 0)

def chain_kernel(SPLITS, PIECE, ROLL, r_ref, wt_ref, lw_ref, ow_ref, cb_ref, out_ref, d_ref, s_ref, top_ref, low_ref, y_ref, *h_refs):
    part = ROWS * W1 // 4
    acc = r_ref[0]
    d_ref[0:4] = jnp.zeros((4, 3 * part), f32)
    d_ref[4:8] = acc
    for n in range(1, N - 1):
        acc = acc + r_ref[n]
        d_ref[4 * n + 4:4 * n + 8] = acc
    field = lax.broadcasted_iota(jnp.int32, (128, 128), 1) & 3
    for t in range(part // 128):
        turned = [d_ref[:, f * part + t * 128:f * part + t * 128 + 128].T for f in range(3)]
        turned = [jnp.concatenate([x, x], axis=1) for x in turned]
        for u in range(4):
            s = jnp.zeros((128, 128), f32)
            for f in range(3):
                moved = turned[f] if f == u else pltpu.roll(turned[f], (f - u) % 128, 1)
                s = jnp.where(field == f, moved, s)
            s_ref[u * part + t * 128:u * part + t * 128 + 128, :] = s
    krow = lax.broadcasted_iota(jnp.int32, (256, 256), 0)
    kslot = (krow & 63) >> 2
    ocol = (lax.broadcasted_iota(jnp.int32, (256, 128), 1) & 63) >> 2
    lw, ow = lw_ref[...].astype(f32), ow_ref[...].astype(f32)

    def rows_of(row, n, pitch):
        if pitch == W1:
            return [pl.ds(row * W1, n * W1)]
        return [pl.ds((row + i) * W1 + (W1 - pitch) // 2, pitch) for i in range(n)]

    def pitch_of(m):
        return W1 if m < 8 else W2

    def lift(m, lo, hi):
        if hi <= lo:
            return
        n, pitch, h = hi - lo, pitch_of(m), h_refs[m % 2]
        cells = n * pitch
        s = jnp.concatenate([s_ref[d, :] for d in rows_of(lo, n, pitch)], axis=0)
        lane = lax.broadcasted_iota(jnp.int32, s.shape, 1)
        lwm = jnp.where((kslot == m) | (krow >= 192), lw, 0.0).astype(bf16)
        y = twice_gelu(jnp.dot(lift_operand(s, lane), lwm, preferred_element_type=f32))
        y_ref[8:8 + cells, :] = y
        left, right = y_ref[7:7 + cells, :], y_ref[9:9 + cells, :]
        dst = pl.ds(lo * pitch, cells)
        h[dst, 0:256] = left.astype(bf16)
        h[dst, 256:512] = y.astype(bf16)
        h[dst, 512:768] = right.astype(bf16)

    def conv(m, lo, hi):
        n, pitch, h = hi - lo, pitch_of(m), h_refs[m % 2]
        x = jnp.concatenate([h[pl.ds((lo + di - 1) * pitch, n * pitch), :] for di in range(3)], axis=1)
        return jnp.dot(x, wt_ref[...].reshape(2304, 256), preferred_element_type=f32)

    def finish(m, lo, hi, acc):
        n, pitch = hi - lo, pitch_of(m)
        act = twice_gelu(acc + cb_ref[...]).astype(bf16)
        owm = jnp.where(ocol >= m, ow, 0.0).astype(bf16)
        inc = jnp.dot(act, owm, preferred_element_type=f32)
        at = 0
        for d in rows_of(lo, n, pitch):
            s_ref[d, :] = s_ref[d, :] + inc[at:at + d.size]
            at += d.size

    def finish_lift(m, lo, hi, acc_ref):
        pitch, h = pitch_of(m), h_refs[(m + 1) % 2]
        lwm = jnp.where((kslot == m + 1) | (krow >= 192), lw, 0.0).astype(bf16)
        owm = jnp.where(ocol >= m, ow, 0.0).astype(bf16)
        count = max(1, round((hi - lo) * pitch / PIECE))
        cuts = [lo + (hi - lo) * i // count for i in range(count + 1)]
        for p, (at, end) in enumerate(zip(cuts[:-1], cuts[1:])):
            if end <= at:
                continue
            cells, base = (end - at) * pitch, (at - lo) * pitch
            act = twice_gelu(acc_ref[base:base + cells, :] + cb_ref[...]).astype(bf16)
            inc = jnp.dot(act, owm, preferred_element_type=f32)
            news, off = [], 0
            for d in rows_of(at, end - at, pitch):
                new = s_ref[d, :] + inc[off:off + d.size]
                s_ref[d, :] = new
                news.append(new)
                off += d.size
            s = jnp.concatenate(news, axis=0)
            lane = lax.broadcasted_iota(jnp.int32, s.shape, 1)
            y = twice_gelu(jnp.dot(lift_operand(s, lane), lwm, preferred_element_type=f32))
            dst = pl.ds(at * pitch, cells)
            if ROLL:
                left, right = shifted(y, cells)
            else:
                top = 8 + at * pitch + 16 * p
                y_ref[top:top + cells, :] = y
                left, right = y_ref[top - 1:top - 1 + cells, :], y_ref[top + 1:top + 1 + cells, :]
            h[dst, 0:256] = left.astype(bf16)
            h[dst, 256:512] = y.astype(bf16)
            h[dst, 512:768] = right.astype(bf16)

    splits = SPLITS

    def block(body):
        body()

    def store_conv(m, lo, hi, acc_ref):
        if hi > lo:
            acc_ref[0:(hi - lo) * pitch_of(m), :] = conv(m, lo, hi)

    def finish_from(m, lo, hi, acc_ref):
        if hi > lo:
            finish(m, lo, hi, acc_ref[0:(hi - lo) * pitch_of(m), :])

    def fits(m, lo, hi, row, end):
        return m + 1 < N and pitch_of(m + 1) == pitch_of(m) and row == lo and end == hi

    lift(1, 0, splits[1] + 1)
    done = splits[1] + 1
    pending = None
    for m in range(1, N):
        lo, hi, b = m, 32 - m, min(splits[m], 32 - m)
        need = b + 1
        if done < need:
            if pending:
                finish_from(*pending, low_ref)
                pending = None
            lift(m, done, need)
            done = need
        store_conv(m, lo, b, top_ref)
        if pending and fits(*pending, done, hi + 1):
            finish_lift(*pending, low_ref)
        else:
            if pending:
                finish_from(*pending, low_ref)
            lift(m, done, hi + 1)
        pending = (m, b, hi)
        early = m if m + 1 == N else max(m, min(b, splits[m + 1] + 1))
        store_conv(m, b, hi, low_ref)
        if b > lo and fits(m, lo, b, m, early):
            finish_lift(m, lo, b, top_ref)
        else:
            finish_from(m, lo, b, top_ref)
            if m + 1 < N:
                lift(m + 1, m, early)
        done = early
    finish_from(*pending, low_ref)
    g = jnp.concatenate([s_ref[15 * W1 + 16:15 * W1 + 32, :], s_ref[16 * W1 + 16:16 * W1 + 32, :]], axis=0)
    gt = g.T
    for n in range(N):
        for f in range(3):
            out_ref[n, :, 32 * f:32 * f + 32] = gt[4 * n + f:4 * n + f + 1, :]
        out_ref[n, :, 96:128] = jnp.zeros((1, 32), f32)

SPLITS = (0, 19, 18, 17, 16, 15, 14, 13, 17, 16, 15, 14, 20, 19, 18, 17)

def chain(recv, wt, lw, ow, cb, SPLITS=SPLITS, PIECE=384, ROLL=False):
    L = ROWS * W1
    vm = pl.BlockSpec(memory_space=pltpu.VMEM)
    return pl.pallas_call(
        functools.partial(chain_kernel, tuple(SPLITS), PIECE, ROLL),
        out_shape=jax.ShapeDtypeStruct((N, 1, 128), f32),
        in_specs=[vm] * 5, out_specs=vm,
        scratch_shapes=[pltpu.VMEM((64, 3 * L // 4), f32), pltpu.VMEM((L, 128), f32), pltpu.VMEM((L, 256), f32), pltpu.VMEM((L, 256), f32), pltpu.VMEM((L + 16 * 16, 256), f32),
                        pltpu.VMEM((L, 768), bf16), pltpu.VMEM((L, 768), bf16)],
        compiler_params=pltpu.CompilerParams(vmem_limit_bytes=48 * 2**20),
    )(recv, wt, lw, ow, cb)

def table_kernel(lwt_ref, lb_ref, cw_ref, ow_ref, wt_ref, lw_ref, owr_ref, wide_ref, rows_ref):
    for i in range(3):
        for j in range(3):
            wt_ref[i, 256 * j:256 * j + 256, :] = (0.5 * cw_ref[i, j].astype(f32)).T.astype(bf16)
    wide_ref[...] = jnp.zeros(wide_ref.shape, f32)
    wide_ref[:, 0:3] = lwt_ref[...]
    w = wide_ref[...].T[0:8]
    hi = w.astype(bf16).astype(f32)
    rows_ref[0:8, :] = hi
    rows_ref[8:16, :] = w - hi
    b = lb_ref[...]
    bhi = b.astype(bf16).astype(f32)
    rows_ref[3:4, :] = bhi
    rows_ref[11:12, :] = b - bhi
    k = lax.broadcasted_iota(jnp.int32, (256, 16), 0)
    col = lax.broadcasted_iota(jnp.int32, (256, 16), 1)
    field = k & 3
    weight = (k < 192) & (field < 3) & (col == field + jnp.where(k < 128, 0, 8))
    bias = ((k == 192) & (col == 3)) | ((k == 193) & (col == 11))
    pick = jnp.where(weight | bias, 1.0, 0.0).astype(bf16)
    lw_ref[...] = jnp.dot(pick, rows_ref[...].astype(bf16), preferred_element_type=f32).astype(bf16)
    rows_ref[...] = jnp.zeros(rows_ref.shape, f32)
    rows_ref[0:3, :] = 0.5 * ow_ref[...].astype(f32)
    lane = lax.broadcasted_iota(jnp.int32, (128, 16), 0) & 3
    pick = jnp.where((lane < 3) & (lane == lax.broadcasted_iota(jnp.int32, (128, 16), 1)), 1.0, 0.0).astype(bf16)
    owr_ref[...] = jnp.dot(pick, rows_ref[...].astype(bf16), preferred_element_type=f32).T.astype(bf16)

def tables(lift_weight, lift_bias, conv_weight, conv_bias, out_weight):
    vm = pl.BlockSpec(memory_space=pltpu.VMEM)
    wt, lw, ow = pl.pallas_call(
        table_kernel,
        out_shape=[jax.ShapeDtypeStruct((3, 768, 256), bf16), jax.ShapeDtypeStruct((256, 256), bf16), jax.ShapeDtypeStruct((256, 128), bf16)],
        in_specs=[vm] * 4, out_specs=[vm] * 3,
        scratch_shapes=[pltpu.VMEM((256, 128), f32), pltpu.VMEM((16, 256), f32)],
        compiler_params=pltpu.CompilerParams(vmem_limit_bytes=32 * 2**20),
        cost_estimate=pl.CostEstimate(flops=10**7, bytes_accessed=10**7, transcendentals=0), name="tables",
    )(lift_weight, lift_bias[None], conv_weight, out_weight)
    return wt, lw, ow, conv_bias[None]

def thirds(x):
    hi = x.astype(bf16)
    rest = x - hi.astype(f32)
    mid = rest.astype(bf16)
    low = (rest - mid.astype(f32)).astype(bf16)
    return jnp.concatenate([hi, mid, low], axis=0)

def exact_dot(x, pattern):
    n = x.shape[0]
    y = jnp.dot(thirds(x), pattern, preferred_element_type=f32)
    return y[0:n] + y[n:2 * n] + y[2 * n:3 * n]

def fine_step(a, b, q):
    def parts(x):
        e, w = pltpu.roll(x, x.shape[1] - 1, 1), pltpu.roll(x, 1, 1)
        n, s = pltpu.roll(x, 1, 0), pltpu.roll(x, x.shape[0] - 1, 0)
        return e - w, s - n, (e + w) + (n + s)
    ax, ay, al = parts(a)
    bx, by, bl = parts(b)
    qx, qy, ql = parts(q)
    half, keep = 0.5 * time_step, 1.0 - 4.0 * time_step * viscosity
    new_a = keep * a + time_step * viscosity * al - half * (a * ax + b * ay + qx)
    new_b = keep * b + time_step * viscosity * bl - half * (a * bx + b * by + qy)
    new_q = keep * q + time_step * viscosity * ql - half * sound_sq * (ax + by)
    return new_a, new_b, new_q

def edge_kernel(s_ref, up_ref, down_ref):
    up_ref[3, 3:4, :] = jnp.zeros((1, s_ref.shape[3]), f32)
    down_ref[3, 3:4, :] = jnp.zeros((1, s_ref.shape[3]), f32)
    for f in range(3):
        up_ref[f] = s_ref[0, f, 12:16, :]
        up_ref[3, f:f + 1, :] = jnp.sum(s_ref[0, f, 8:16, :], axis=0, keepdims=True)
        down_ref[f] = s_ref[0, f, 0:4, :]
        down_ref[3, f:f + 1, :] = jnp.sum(s_ref[0, f, 0:8, :], axis=0, keepdims=True)

def first_kernel(tm_ref, s_ref, up_ref, dn_ref, wt_ref, lw_ref, ow_ref, cb_ref, corr_ref, c_ref, q_ref, qf_ref, h_ref):
    blank = jnp.zeros((4, s_ref.shape[3]), f32)
    fields = [jnp.concatenate([blank, up_ref[f], s_ref[0, f], dn_ref[f], blank], axis=0) for f in range(3)]
    q_ref[...] = jnp.zeros(q_ref.shape, f32)
    qf_ref[...] = jnp.zeros(qf_ref.shape, f32)
    q_ref[0:4, :] = up_ref[3]
    q_ref[12:16, :] = dn_ref[3]
    for f in range(3):
        for r in range(2):
            q_ref[4 + 4 * r + f:5 + 4 * r + f, :] = jnp.sum(s_ref[0, f, 8 * r:8 * r + 8, :], axis=0, keepdims=True)
    half = 128 * RF
    pool = (lax.broadcasted_iota(jnp.int32, (half, 128), 0) // RF == lax.broadcasted_iota(jnp.int32, (half, 128), 1)).astype(f32).astype(bf16)
    spread = (lax.broadcasted_iota(jnp.int32, (128, half), 1) // RF == lax.broadcasted_iota(jnp.int32, (128, half), 0)).astype(f32).astype(bf16)

    def pooled(ref):
        return jnp.concatenate([exact_dot(ref[:, 0:half], pool), exact_dot(ref[:, half:], pool)], axis=1) * (1.0 / (RF * RF))
    start = pooled(q_ref)
    pad = jnp.zeros((48, 256), f32)
    s = jnp.concatenate([start, pad, start, pad], axis=0).T
    x = lift_operand(s, lax.broadcasted_iota(jnp.int32, s.shape, 1))
    krow = lax.broadcasted_iota(jnp.int32, (256, 256), 0)
    kslot = (krow & 63) >> 2
    lw = lw_ref[...].astype(f32)
    fields = fine_step(*fields)
    for r in range(4):
        lwm = jnp.where((kslot == r) | (krow >= 192), lw, 0.0).astype(bf16)
        h = twice_gelu(jnp.dot(x, lwm, preferred_element_type=f32))
        left, right = shifted(h, 256)
        h_ref[256 * r:256 * r + 256, 0:256] = left.astype(bf16)
        h_ref[256 * r:256 * r + 256, 256:512] = h.astype(bf16)
        h_ref[256 * r:256 * r + 256, 512:768] = right.astype(bf16)
    fields = fine_step(*fields)
    acc = jnp.dot(h_ref[0:512], wt_ref[0], preferred_element_type=f32)
    acc = acc + jnp.dot(h_ref[256:768], wt_ref[1], preferred_element_type=f32)
    acc = acc + jnp.dot(h_ref[512:1024], wt_ref[2], preferred_element_type=f32)
    fields = fine_step(*fields)
    act = twice_gelu(acc + cb_ref[...]).astype(bf16)
    inc = jnp.dot(act, ow_ref[...], preferred_element_type=f32)
    lane = lax.broadcasted_iota(jnp.int32, s.shape, 1)
    guess = (s + jnp.where(lane < 8, inc[0:256], inc[256:512])).T[4:12]
    for _ in range(FINE - 3):
        fields = fine_step(*fields)
    for f in range(3):
        for r in range(2):
            qf_ref[4 * r + f:4 * r + f + 1, :] = jnp.sum(fields[f][8 + 8 * r:16 + 8 * r], axis=0, keepdims=True)
    first = jnp.where(tm_ref[0] == 0, guess, 0.0)
    c = first + (pooled(qf_ref) - guess)
    for i in range(c_ref.shape[0]):
        c_ref[i] = c
    delta = guess - first
    for p in range(2):
        wide = exact_dot(delta[:, 128 * p:128 * p + 128], spread)
        for f in range(3):
            for r in range(2):
                corr_ref[f, 8 * r:8 * r + 8, half * p:half * p + half] = fields[f][8 + 8 * r:16 + 8 * r, half * p:half * p + half] - wide[4 * r + f:4 * r + f + 1]

def window_kernel(sp_ref, b_ref, out_ref, w_ref):
    count = b_ref.shape[0]
    for q in range(ROWS):
        dev = lax.rem(sp_ref[0] + (count - 8 + (q + 1) // 2), count)
        r = (q + 1) % 2
        for f in range(3):
            w_ref[3 * (q % 8) + f, q // 8:q // 8 + 1, :] = b_ref[dev, 4 * r + f:4 * r + f + 1, :]
    for i in range(8):
        for f in range(3):
            v = w_ref[3 * i + f]
            ext = jnp.concatenate([v[:, 240:256], v, v[:, 0:16]], axis=1)
            at = f * 8 * W1 + i * W1
            for j in range(N):
                out_ref[j, :, at:at + W1] = ext[:, 16 * j:16 * j + W1]

def last_kernel(g_ref, corr_ref, out_ref, y_ref):
    for j in range(N):
        y_ref[j:j + 1, :] = g_ref[j]
    parts = thirds(y_ref[...])
    row = lax.broadcasted_iota(jnp.int32, (128, 128), 0)
    col = lax.broadcasted_iota(jnp.int32, (128, 128), 1)
    for r in range(2):
        for f in range(3):
            pattern = (row - 32 * f - 16 * r == col // RF).astype(f32).astype(bf16)
            y = jnp.dot(parts, pattern, preferred_element_type=f32)
            y = y[0:N] + y[N:2 * N] + y[2 * N:3 * N]
            for j in range(N):
                at = 128 * j
                out_ref[0, f, 8 * r:8 * r + 8, at:at + 128] = corr_ref[f, 8 * r:8 * r + 8, at:at + 128] + y[j:j + 1]

def shards(start_states, lift_weight, lift_bias, conv_weight, conv_bias, out_weight):
    vm = pl.BlockSpec(memory_space=pltpu.VMEM)
    sm = pl.BlockSpec(memory_space=pltpu.SMEM)
    params = pltpu.CompilerParams(vmem_limit_bytes=48 * 2**20)
    count = lax.axis_size("space")
    slab = start_states[0]
    edges = jax.ShapeDtypeStruct((4, 4, slab.shape[2]), f32)
    up, down = pl.pallas_call(edge_kernel, out_shape=[edges, edges], in_specs=[vm], out_specs=[vm, vm], compiler_params=params, name="edges")(start_states)
    up = lax.ppermute(up, "space", [(i, (i + 1) % count) for i in range(count)])
    down = lax.ppermute(down, "space", [((i + 1) % count, i) for i in range(count)])
    weights = tables(lift_weight, lift_bias, conv_weight, conv_bias, out_weight)
    tm = lax.axis_index("tm").astype(jnp.int32).reshape(1)
    sp = lax.axis_index("space").astype(jnp.int32).reshape(1)
    corr, c = pl.pallas_call(
        first_kernel,
        out_shape=[jax.ShapeDtypeStruct(slab.shape, f32), jax.ShapeDtypeStruct((count, 8, 256), f32)],
        in_specs=[sm] + [vm] * 7, out_specs=[vm, vm],
        scratch_shapes=[pltpu.VMEM((16, slab.shape[2]), f32), pltpu.VMEM((8, slab.shape[2]), f32), pltpu.VMEM((1024, 768), bf16)],
        compiler_params=params, name="fine_and_guess",
    )(tm, start_states, up, down, *weights)
    c = lax.all_to_all(c, "space", 0, 0)
    send = pl.pallas_call(
        window_kernel, out_shape=jax.ShapeDtypeStruct((N, 4, 3 * ROWS * W1 // 4), f32),
        in_specs=[sm, vm], out_specs=vm, scratch_shapes=[pltpu.VMEM((24, 4, 256), f32)],
        compiler_params=params, name="windows",
    )(sp, c)
    recv = lax.all_to_all(send, "tm", 0, 0)
    g = chain(recv, *weights)
    g = lax.all_to_all(g, "tm", 0, 0)
    return pl.pallas_call(
        last_kernel, out_shape=jax.ShapeDtypeStruct(start_states.shape, f32),
        in_specs=[vm, vm], out_specs=vm, scratch_shapes=[pltpu.VMEM((N, 128), f32)],
        compiler_params=params, name="correct",
    )(g, corr)

def solution(mesh):
    return jax.shard_map(
        shards, mesh=mesh,
        in_specs=(P("tm", None, "space", None), P(), P(), P(), P(), P()),
        out_specs=P("tm", None, "space", None), check_vma=False,
    )
```

```python
import functools
import jax, jax.numpy as jnp
from jax import lax
from jax.experimental import pallas as pl
from jax.experimental.pallas import tpu as pltpu
from jax.sharding import PartitionSpec as P

f32, bf16 = jnp.float32, jnp.bfloat16
FINE = 4
RF = 8
time_step = 0.2
viscosity = 1.0
sound_sq = 1.0
N = 16
ROWS = 32
W1, W2 = 48, 32

def twice_gelu(x):
    u = x * (0.7978845608028654 + 0.035677408136300125 * (x * x))
    return x + x * jnp.tanh(u)

def lift_operand(s, lane):
    hi = s.astype(bf16)
    lo = (s - hi.astype(f32)).astype(bf16)
    one = jnp.ones_like(hi)
    return jnp.concatenate([jnp.where(lane < 64, hi, lo), jnp.where(lane < 64, hi, one)], axis=1)

def shifted(h, axis_size):
    return pltpu.roll(h, 1, 0), pltpu.roll(h, axis_size - 1, 0)

def chain_kernel(SPLITS, PIECE, ROLL, r_ref, wt_ref, lw_ref, ow_ref, cb_ref, out_ref, d_ref, s_ref, top_ref, low_ref, y_ref, *h_refs):
    part = ROWS * W1 // 4
    acc = r_ref[0]
    d_ref[0:4] = jnp.zeros((4, 3 * part), f32)
    d_ref[4:8] = acc
    for n in range(1, N - 1):
        acc = acc + r_ref[n]
        d_ref[4 * n + 4:4 * n + 8] = acc
    field = lax.broadcasted_iota(jnp.int32, (128, 128), 1) & 3
    for t in range(part // 128):
        turned = [d_ref[:, f * part + t * 128:f * part + t * 128 + 128].T for f in range(3)]
        turned = [jnp.concatenate([x, x], axis=1) for x in turned]
        for u in range(4):
            s = jnp.zeros((128, 128), f32)
            for f in range(3):
                moved = turned[f] if f == u else pltpu.roll(turned[f], (f - u) % 128, 1)
                s = jnp.where(field == f, moved, s)
            s_ref[u * part + t * 128:u * part + t * 128 + 128, :] = s
    krow = lax.broadcasted_iota(jnp.int32, (256, 256), 0)
    kslot = (krow & 63) >> 2
    ocol = (lax.broadcasted_iota(jnp.int32, (256, 128), 1) & 63) >> 2
    lw, ow = lw_ref[...].astype(f32), ow_ref[...].astype(f32)

    def rows_of(row, n, pitch):
        if pitch == W1:
            return [pl.ds(row * W1, n * W1)]
        return [pl.ds((row + i) * W1 + (W1 - pitch) // 2, pitch) for i in range(n)]

    def pitch_of(m):
        return W1 if m < 8 else W2

    def lift(m, lo, hi):
        if hi <= lo:
            return
        n, pitch, h = hi - lo, pitch_of(m), h_refs[m % 2]
        cells = n * pitch
        s = jnp.concatenate([s_ref[d, :] for d in rows_of(lo, n, pitch)], axis=0)
        lane = lax.broadcasted_iota(jnp.int32, s.shape, 1)
        lwm = jnp.where((kslot == m) | (krow >= 192), lw, 0.0).astype(bf16)
        y = twice_gelu(jnp.dot(lift_operand(s, lane), lwm, preferred_element_type=f32))
        y_ref[8:8 + cells, :] = y
        left, right = y_ref[7:7 + cells, :], y_ref[9:9 + cells, :]
        dst = pl.ds(lo * pitch, cells)
        h[dst, 0:256] = left.astype(bf16)
        h[dst, 256:512] = y.astype(bf16)
        h[dst, 512:768] = right.astype(bf16)

    def conv(m, lo, hi):
        n, pitch, h = hi - lo, pitch_of(m), h_refs[m % 2]
        x = jnp.concatenate([h[pl.ds((lo + di - 1) * pitch, n * pitch), :] for di in range(3)], axis=1)
        return jnp.dot(x, wt_ref[...].reshape(2304, 256), preferred_element_type=f32)

    def finish(m, lo, hi, acc):
        n, pitch = hi - lo, pitch_of(m)
        act = twice_gelu(acc + cb_ref[...]).astype(bf16)
        owm = jnp.where(ocol >= m, ow, 0.0).astype(bf16)
        inc = jnp.dot(act, owm, preferred_element_type=f32)
        at = 0
        for d in rows_of(lo, n, pitch):
            s_ref[d, :] = s_ref[d, :] + inc[at:at + d.size]
            at += d.size

    def finish_lift(m, lo, hi, acc_ref):
        pitch, h = pitch_of(m), h_refs[(m + 1) % 2]
        lwm = jnp.where((kslot == m + 1) | (krow >= 192), lw, 0.0).astype(bf16)
        owm = jnp.where(ocol >= m, ow, 0.0).astype(bf16)
        count = max(1, round((hi - lo) * pitch / PIECE))
        cuts = [lo + (hi - lo) * i // count for i in range(count + 1)]
        for p, (at, end) in enumerate(zip(cuts[:-1], cuts[1:])):
            if end <= at:
                continue
            cells, base = (end - at) * pitch, (at - lo) * pitch
            act = twice_gelu(acc_ref[base:base + cells, :] + cb_ref[...]).astype(bf16)
            inc = jnp.dot(act, owm, preferred_element_type=f32)
            news, off = [], 0
            for d in rows_of(at, end - at, pitch):
                new = s_ref[d, :] + inc[off:off + d.size]
                s_ref[d, :] = new
                news.append(new)
                off += d.size
            s = jnp.concatenate(news, axis=0)
            lane = lax.broadcasted_iota(jnp.int32, s.shape, 1)
            y = twice_gelu(jnp.dot(lift_operand(s, lane), lwm, preferred_element_type=f32))
            dst = pl.ds(at * pitch, cells)
            if ROLL:
                left, right = shifted(y, cells)
            else:
                top = 8 + at * pitch + 16 * p
                y_ref[top:top + cells, :] = y
                left, right = y_ref[top - 1:top - 1 + cells, :], y_ref[top + 1:top + 1 + cells, :]
            h[dst, 0:256] = left.astype(bf16)
            h[dst, 256:512] = y.astype(bf16)
            h[dst, 512:768] = right.astype(bf16)

    splits = SPLITS

    def block(body):
        body()

    def store_conv(m, lo, hi, acc_ref):
        if hi > lo:
            acc_ref[0:(hi - lo) * pitch_of(m), :] = conv(m, lo, hi)

    def finish_from(m, lo, hi, acc_ref):
        if hi > lo:
            finish(m, lo, hi, acc_ref[0:(hi - lo) * pitch_of(m), :])

    def fits(m, lo, hi, row, end):
        return m + 1 < N and pitch_of(m + 1) == pitch_of(m) and row == lo and end == hi

    lift(1, 0, splits[1] + 1)
    done = splits[1] + 1
    pending = None
    for m in range(1, N):
        lo, hi, b = m, 32 - m, min(splits[m], 32 - m)
        need = b + 1
        if done < need:
            if pending:
                finish_from(*pending, low_ref)
                pending = None
            lift(m, done, need)
            done = need
        store_conv(m, lo, b, top_ref)
        if pending and fits(*pending, done, hi + 1):
            finish_lift(*pending, low_ref)
        else:
            if pending:
                finish_from(*pending, low_ref)
            lift(m, done, hi + 1)
        pending = (m, b, hi)
        early = m if m + 1 == N else max(m, min(b, splits[m + 1] + 1))
        store_conv(m, b, hi, low_ref)
        if b > lo and fits(m, lo, b, m, early):
            finish_lift(m, lo, b, top_ref)
        else:
            finish_from(m, lo, b, top_ref)
            if m + 1 < N:
                lift(m + 1, m, early)
        done = early
    finish_from(*pending, low_ref)
    g = jnp.concatenate([s_ref[15 * W1 + 16:15 * W1 + 32, :], s_ref[16 * W1 + 16:16 * W1 + 32, :]], axis=0)
    gt = g.T
    for n in range(N):
        for f in range(3):
            out_ref[n, :, 32 * f:32 * f + 32] = gt[4 * n + f:4 * n + f + 1, :]
        out_ref[n, :, 96:128] = jnp.zeros((1, 32), f32)

SPLITS = (0, 19, 18, 17, 16, 15, 14, 13, 17, 16, 15, 14, 20, 19, 18, 17)

def chain(recv, wt, lw, ow, cb, SPLITS=SPLITS, PIECE=384, ROLL=False):
    L = ROWS * W1
    vm = pl.BlockSpec(memory_space=pltpu.VMEM)
    return pl.pallas_call(
        functools.partial(chain_kernel, tuple(SPLITS), PIECE, ROLL),
        out_shape=jax.ShapeDtypeStruct((N, 1, 128), f32),
        in_specs=[vm] * 5, out_specs=vm,
        scratch_shapes=[pltpu.VMEM((64, 3 * L // 4), f32), pltpu.VMEM((L, 128), f32), pltpu.VMEM((L, 256), f32), pltpu.VMEM((L, 256), f32), pltpu.VMEM((L + 16 * 16, 256), f32),
                        pltpu.VMEM((L, 768), bf16), pltpu.VMEM((L, 768), bf16)],
        compiler_params=pltpu.CompilerParams(vmem_limit_bytes=48 * 2**20),
    )(recv, wt, lw, ow, cb)

def table_kernel(cw_ref, small_ref, wt_ref, lw_ref, owr_ref, rows_ref):
    for i in range(3):
        for j in range(3):
            wt_ref[i, 256 * j:256 * j + 256, :] = (0.5 * cw_ref[i, j].astype(f32)).T.astype(bf16)
    rows_ref[...] = jnp.zeros(rows_ref.shape, f32)
    w = small_ref[0:3, :]
    hi = w.astype(bf16).astype(f32)
    rows_ref[0:3, :] = hi
    rows_ref[8:11, :] = w - hi
    b = small_ref[3:4, :]
    bhi = b.astype(bf16).astype(f32)
    rows_ref[3:4, :] = bhi
    rows_ref[11:12, :] = b - bhi
    k = lax.broadcasted_iota(jnp.int32, (256, 16), 0)
    col = lax.broadcasted_iota(jnp.int32, (256, 16), 1)
    field = k & 3
    weight = (k < 192) & (field < 3) & (col == field + jnp.where(k < 128, 0, 8))
    bias = ((k == 192) & (col == 3)) | ((k == 193) & (col == 11))
    pick = jnp.where(weight | bias, 1.0, 0.0).astype(bf16)
    lw_ref[...] = jnp.dot(pick, rows_ref[...].astype(bf16), preferred_element_type=f32).astype(bf16)
    rows_ref[...] = jnp.zeros(rows_ref.shape, f32)
    rows_ref[0:3, :] = 0.5 * small_ref[4:7, :]
    lane = lax.broadcasted_iota(jnp.int32, (128, 16), 0) & 3
    pick = jnp.where((lane < 3) & (lane == lax.broadcasted_iota(jnp.int32, (128, 16), 1)), 1.0, 0.0).astype(bf16)
    owr_ref[...] = jnp.dot(pick, rows_ref[...].astype(bf16), preferred_element_type=f32).T.astype(bf16)

def tables(lift_weight, lift_bias, conv_weight, conv_bias, out_weight):
    vm = pl.BlockSpec(memory_space=pltpu.VMEM)
    wt, lw, ow = pl.pallas_call(
        table_kernel,
        out_shape=[jax.ShapeDtypeStruct((3, 768, 256), bf16), jax.ShapeDtypeStruct((256, 256), bf16), jax.ShapeDtypeStruct((256, 128), bf16)],
        in_specs=[vm] * 2, out_specs=[vm] * 3,
        scratch_shapes=[pltpu.VMEM((16, 256), f32)],
        compiler_params=pltpu.CompilerParams(vmem_limit_bytes=32 * 2**20),
        cost_estimate=pl.CostEstimate(flops=10**7, bytes_accessed=10**7, transcendentals=0), name="tables",
    )(conv_weight, jnp.concatenate([lift_weight.T, lift_bias[None], out_weight.astype(f32)], axis=0))
    return wt, lw, ow, conv_bias[None]

def thirds(x):
    hi = x.astype(bf16)
    rest = x - hi.astype(f32)
    mid = rest.astype(bf16)
    low = (rest - mid.astype(f32)).astype(bf16)
    return jnp.concatenate([hi, mid, low], axis=0)

def exact_dot(x, pattern):
    n = x.shape[0]
    y = jnp.dot(thirds(x), pattern, preferred_element_type=f32)
    return y[0:n] + y[n:2 * n] + y[2 * n:3 * n]

def fine_step(a, b, q):
    def parts(x):
        e, w = pltpu.roll(x, x.shape[1] - 1, 1), pltpu.roll(x, 1, 1)
        n, s = pltpu.roll(x, 1, 0), pltpu.roll(x, x.shape[0] - 1, 0)
        return e - w, s - n, (e + w) + (n + s)
    ax, ay, al = parts(a)
    bx, by, bl = parts(b)
    qx, qy, ql = parts(q)
    half, keep = 0.5 * time_step, 1.0 - 4.0 * time_step * viscosity
    new_a = keep * a + time_step * viscosity * al - half * (a * ax + b * ay + qx)
    new_b = keep * b + time_step * viscosity * bl - half * (a * bx + b * by + qy)
    new_q = keep * q + time_step * viscosity * ql - half * sound_sq * (ax + by)
    return new_a, new_b, new_q

def edge_kernel(s_ref, up_ref, down_ref):
    up_ref[3, 3:4, :] = jnp.zeros((1, s_ref.shape[3]), f32)
    down_ref[3, 3:4, :] = jnp.zeros((1, s_ref.shape[3]), f32)
    for f in range(3):
        up_ref[f] = s_ref[0, f, 12:16, :]
        up_ref[3, f:f + 1, :] = jnp.sum(s_ref[0, f, 8:16, :], axis=0, keepdims=True)
        down_ref[f] = s_ref[0, f, 0:4, :]
        down_ref[3, f:f + 1, :] = jnp.sum(s_ref[0, f, 0:8, :], axis=0, keepdims=True)

def first_kernel(tm_ref, s_ref, up_ref, dn_ref, wt_ref, lw_ref, ow_ref, cb_ref, corr_ref, c_ref, q_ref, qf_ref, h_ref):
    blank = jnp.zeros((4, s_ref.shape[3]), f32)
    fields = [jnp.concatenate([blank, up_ref[f], s_ref[0, f], dn_ref[f], blank], axis=0) for f in range(3)]
    q_ref[...] = jnp.zeros(q_ref.shape, f32)
    qf_ref[...] = jnp.zeros(qf_ref.shape, f32)
    q_ref[0:4, :] = up_ref[3]
    q_ref[12:16, :] = dn_ref[3]
    for f in range(3):
        for r in range(2):
            q_ref[4 + 4 * r + f:5 + 4 * r + f, :] = jnp.sum(s_ref[0, f, 8 * r:8 * r + 8, :], axis=0, keepdims=True)
    half = 128 * RF
    pool = (lax.broadcasted_iota(jnp.int32, (half, 128), 0) // RF == lax.broadcasted_iota(jnp.int32, (half, 128), 1)).astype(f32).astype(bf16)
    spread = (lax.broadcasted_iota(jnp.int32, (128, half), 1) // RF == lax.broadcasted_iota(jnp.int32, (128, half), 0)).astype(f32).astype(bf16)

    def pooled(ref):
        return jnp.concatenate([exact_dot(ref[:, 0:half], pool), exact_dot(ref[:, half:], pool)], axis=1) * (1.0 / (RF * RF))
    start = pooled(q_ref)
    pad = jnp.zeros((48, 256), f32)
    s = jnp.concatenate([start, pad, start, pad], axis=0).T
    x = lift_operand(s, lax.broadcasted_iota(jnp.int32, s.shape, 1))
    krow = lax.broadcasted_iota(jnp.int32, (256, 256), 0)
    kslot = (krow & 63) >> 2
    lw = lw_ref[...].astype(f32)
    fields = fine_step(*fields)
    for r in range(4):
        lwm = jnp.where((kslot == r) | (krow >= 192), lw, 0.0).astype(bf16)
        h = twice_gelu(jnp.dot(x, lwm, preferred_element_type=f32))
        left, right = shifted(h, 256)
        h_ref[256 * r:256 * r + 256, 0:256] = left.astype(bf16)
        h_ref[256 * r:256 * r + 256, 256:512] = h.astype(bf16)
        h_ref[256 * r:256 * r + 256, 512:768] = right.astype(bf16)
    fields = fine_step(*fields)
    acc = jnp.dot(h_ref[0:512], wt_ref[0], preferred_element_type=f32)
    acc = acc + jnp.dot(h_ref[256:768], wt_ref[1], preferred_element_type=f32)
    acc = acc + jnp.dot(h_ref[512:1024], wt_ref[2], preferred_element_type=f32)
    fields = fine_step(*fields)
    act = twice_gelu(acc + cb_ref[...]).astype(bf16)
    inc = jnp.dot(act, ow_ref[...], preferred_element_type=f32)
    lane = lax.broadcasted_iota(jnp.int32, s.shape, 1)
    guess = (s + jnp.where(lane < 8, inc[0:256], inc[256:512])).T[4:12]
    for _ in range(FINE - 3):
        fields = fine_step(*fields)
    for f in range(3):
        for r in range(2):
            qf_ref[4 * r + f:4 * r + f + 1, :] = jnp.sum(fields[f][8 + 8 * r:16 + 8 * r], axis=0, keepdims=True)
    first = jnp.where(tm_ref[0] == 0, guess, 0.0)
    c = first + (pooled(qf_ref) - guess)
    for i in range(c_ref.shape[0]):
        c_ref[i] = c
    delta = guess - first
    for p in range(2):
        wide = exact_dot(delta[:, 128 * p:128 * p + 128], spread)
        for f in range(3):
            for r in range(2):
                corr_ref[f, 8 * r:8 * r + 8, half * p:half * p + half] = fields[f][8 + 8 * r:16 + 8 * r, half * p:half * p + half] - wide[4 * r + f:4 * r + f + 1]

def window_kernel(sp_ref, b_ref, out_ref, w_ref):
    count = b_ref.shape[0]
    for q in range(ROWS):
        dev = lax.rem(sp_ref[0] + (count - 8 + (q + 1) // 2), count)
        r = (q + 1) % 2
        for f in range(3):
            w_ref[3 * (q % 8) + f, q // 8:q // 8 + 1, :] = b_ref[dev, 4 * r + f:4 * r + f + 1, :]
    for i in range(8):
        for f in range(3):
            v = w_ref[3 * i + f]
            ext = jnp.concatenate([v[:, 240:256], v, v[:, 0:16]], axis=1)
            at = f * 8 * W1 + i * W1
            for j in range(N):
                out_ref[j, :, at:at + W1] = ext[:, 16 * j:16 * j + W1]

def last_kernel(g_ref, corr_ref, out_ref, y_ref):
    for j in range(N):
        y_ref[j:j + 1, :] = g_ref[j]
    parts = thirds(y_ref[...])
    row = lax.broadcasted_iota(jnp.int32, (128, 128), 0)
    col = lax.broadcasted_iota(jnp.int32, (128, 128), 1)
    for r in range(2):
        for f in range(3):
            pattern = (row - 32 * f - 16 * r == col // RF).astype(f32).astype(bf16)
            y = jnp.dot(parts, pattern, preferred_element_type=f32)
            y = y[0:N] + y[N:2 * N] + y[2 * N:3 * N]
            for j in range(N):
                at = 128 * j
                out_ref[0, f, 8 * r:8 * r + 8, at:at + 128] = corr_ref[f, 8 * r:8 * r + 8, at:at + 128] + y[j:j + 1]

def shards(start_states, lift_weight, lift_bias, conv_weight, conv_bias, out_weight):
    vm = pl.BlockSpec(memory_space=pltpu.VMEM)
    sm = pl.BlockSpec(memory_space=pltpu.SMEM)
    params = pltpu.CompilerParams(vmem_limit_bytes=48 * 2**20)
    count = lax.axis_size("space")
    slab = start_states[0]
    edges = jax.ShapeDtypeStruct((4, 4, slab.shape[2]), f32)
    up, down = pl.pallas_call(edge_kernel, out_shape=[edges, edges], in_specs=[vm], out_specs=[vm, vm], compiler_params=params, name="edges")(start_states)
    up = lax.ppermute(up, "space", [(i, (i + 1) % count) for i in range(count)])
    down = lax.ppermute(down, "space", [((i + 1) % count, i) for i in range(count)])
    weights = tables(lift_weight, lift_bias, conv_weight, conv_bias, out_weight)
    tm = lax.axis_index("tm").astype(jnp.int32).reshape(1)
    sp = lax.axis_index("space").astype(jnp.int32).reshape(1)
    corr, c = pl.pallas_call(
        first_kernel,
        out_shape=[jax.ShapeDtypeStruct(slab.shape, f32), jax.ShapeDtypeStruct((count, 8, 256), f32)],
        in_specs=[sm] + [vm] * 7, out_specs=[vm, vm],
        scratch_shapes=[pltpu.VMEM((16, slab.shape[2]), f32), pltpu.VMEM((8, slab.shape[2]), f32), pltpu.VMEM((1024, 768), bf16)],
        compiler_params=params, name="fine_and_guess",
    )(tm, start_states, up, down, *weights)
    c = lax.all_to_all(c, "space", 0, 0)
    send = pl.pallas_call(
        window_kernel, out_shape=jax.ShapeDtypeStruct((N, 4, 3 * ROWS * W1 // 4), f32),
        in_specs=[sm, vm], out_specs=vm, scratch_shapes=[pltpu.VMEM((24, 4, 256), f32)],
        compiler_params=params, name="windows",
    )(sp, c)
    recv = lax.all_to_all(send, "tm", 0, 0)
    g = chain(recv, *weights)
    g = lax.all_to_all(g, "tm", 0, 0)
    return pl.pallas_call(
        last_kernel, out_shape=jax.ShapeDtypeStruct(start_states.shape, f32),
        in_specs=[vm, vm], out_specs=vm, scratch_shapes=[pltpu.VMEM((N, 128), f32)],
        compiler_params=params, name="correct",
    )(g, corr)

def solution(mesh):
    return jax.shard_map(
        shards, mesh=mesh,
        in_specs=(P("tm", None, "space", None), P(), P(), P(), P(), P()),
        out_specs=P("tm", None, "space", None), check_vma=False,
    )
```

```python
import functools
import jax, jax.numpy as jnp
from jax import lax
from jax.experimental import pallas as pl
from jax.experimental.pallas import tpu as pltpu
from jax.sharding import PartitionSpec as P

f32, bf16 = jnp.float32, jnp.bfloat16
FINE = 4
RF = 8
time_step = 0.2
viscosity = 1.0
sound_sq = 1.0
N = 16
ROWS = 32
W1, W2 = 48, 32

def twice_gelu(x):
    u = x * (0.7978845608028654 + 0.035677408136300125 * (x * x))
    return x + x * jnp.tanh(u)

def lift_operand(s, lane):
    hi = s.astype(bf16)
    lo = (s - hi.astype(f32)).astype(bf16)
    one = jnp.ones_like(hi)
    return jnp.concatenate([jnp.where(lane < 64, hi, lo), jnp.where(lane < 64, hi, one)], axis=1)

def shifted(h, axis_size):
    return pltpu.roll(h, 1, 0), pltpu.roll(h, axis_size - 1, 0)

def chain_kernel(SPLITS, PIECE, ROLL, r_ref, wt_ref, lw_ref, ow_ref, cb_ref, out_ref, d_ref, s_ref, top_ref, low_ref, y_ref, *h_refs):
    part = ROWS * W1 // 4
    acc = r_ref[0]
    d_ref[0:4] = jnp.zeros((4, 3 * part), f32)
    d_ref[4:8] = acc
    for n in range(1, N - 1):
        acc = acc + r_ref[n]
        d_ref[4 * n + 4:4 * n + 8] = acc
    field = lax.broadcasted_iota(jnp.int32, (128, 128), 1) & 3
    for t in range(part // 128):
        turned = [d_ref[:, f * part + t * 128:f * part + t * 128 + 128].T for f in range(3)]
        turned = [jnp.concatenate([x, x], axis=1) for x in turned]
        for u in range(4):
            s = jnp.zeros((128, 128), f32)
            for f in range(3):
                moved = turned[f] if f == u else pltpu.roll(turned[f], (f - u) % 128, 1)
                s = jnp.where(field == f, moved, s)
            s_ref[u * part + t * 128:u * part + t * 128 + 128, :] = s
    krow = lax.broadcasted_iota(jnp.int32, (256, 256), 0)
    kslot = (krow & 63) >> 2
    ocol = (lax.broadcasted_iota(jnp.int32, (256, 128), 1) & 63) >> 2
    lw, ow = lw_ref[...].astype(f32), ow_ref[...].astype(f32)

    def rows_of(row, n, pitch):
        if pitch == W1:
            return [pl.ds(row * W1, n * W1)]
        return [pl.ds((row + i) * W1 + (W1 - pitch) // 2, pitch) for i in range(n)]

    def pitch_of(m):
        return W1 if m < 8 else W2

    def lift(m, lo, hi):
        if hi <= lo:
            return
        n, pitch, h = hi - lo, pitch_of(m), h_refs[m % 2]
        cells = n * pitch
        s = jnp.concatenate([s_ref[d, :] for d in rows_of(lo, n, pitch)], axis=0)
        lane = lax.broadcasted_iota(jnp.int32, s.shape, 1)
        lwm = jnp.where((kslot == m) | (krow >= 192), lw, 0.0).astype(bf16)
        y = twice_gelu(jnp.dot(lift_operand(s, lane), lwm, preferred_element_type=f32))
        y_ref[8:8 + cells, :] = y
        left, right = y_ref[7:7 + cells, :], y_ref[9:9 + cells, :]
        dst = pl.ds(lo * pitch, cells)
        h[dst, 0:256] = left.astype(bf16)
        h[dst, 256:512] = y.astype(bf16)
        h[dst, 512:768] = right.astype(bf16)

    def conv(m, lo, hi):
        n, pitch, h = hi - lo, pitch_of(m), h_refs[m % 2]
        x = jnp.concatenate([h[pl.ds((lo + di - 1) * pitch, n * pitch), :] for di in range(3)], axis=1)
        return jnp.dot(x, wt_ref[...].reshape(2304, 256), preferred_element_type=f32)

    def finish(m, lo, hi, acc):
        n, pitch = hi - lo, pitch_of(m)
        act = twice_gelu(acc + cb_ref[...]).astype(bf16)
        owm = jnp.where(ocol >= m, ow, 0.0).astype(bf16)
        inc = jnp.dot(act, owm, preferred_element_type=f32)
        at = 0
        for d in rows_of(lo, n, pitch):
            s_ref[d, :] = s_ref[d, :] + inc[at:at + d.size]
            at += d.size

    def finish_lift(m, lo, hi, acc_ref):
        pitch, h = pitch_of(m), h_refs[(m + 1) % 2]
        lwm = jnp.where((kslot == m + 1) | (krow >= 192), lw, 0.0).astype(bf16)
        owm = jnp.where(ocol >= m, ow, 0.0).astype(bf16)
        count = max(1, round((hi - lo) * pitch / PIECE))
        cuts = [lo + (hi - lo) * i // count for i in range(count + 1)]
        for p, (at, end) in enumerate(zip(cuts[:-1], cuts[1:])):
            if end <= at:
                continue
            cells, base = (end - at) * pitch, (at - lo) * pitch
            act = twice_gelu(acc_ref[base:base + cells, :] + cb_ref[...]).astype(bf16)
            inc = jnp.dot(act, owm, preferred_element_type=f32)
            news, off = [], 0
            for d in rows_of(at, end - at, pitch):
                new = s_ref[d, :] + inc[off:off + d.size]
                s_ref[d, :] = new
                news.append(new)
                off += d.size
            s = jnp.concatenate(news, axis=0)
            lane = lax.broadcasted_iota(jnp.int32, s.shape, 1)
            y = twice_gelu(jnp.dot(lift_operand(s, lane), lwm, preferred_element_type=f32))
            dst = pl.ds(at * pitch, cells)
            if ROLL:
                left, right = shifted(y, cells)
            else:
                top = 8 + at * pitch + 16 * p
                y_ref[top:top + cells, :] = y
                left, right = y_ref[top - 1:top - 1 + cells, :], y_ref[top + 1:top + 1 + cells, :]
            h[dst, 0:256] = left.astype(bf16)
            h[dst, 256:512] = y.astype(bf16)
            h[dst, 512:768] = right.astype(bf16)

    splits = SPLITS

    def block(body):
        body()

    def store_conv(m, lo, hi, acc_ref):
        if hi > lo:
            acc_ref[0:(hi - lo) * pitch_of(m), :] = conv(m, lo, hi)

    def finish_from(m, lo, hi, acc_ref):
        if hi > lo:
            finish(m, lo, hi, acc_ref[0:(hi - lo) * pitch_of(m), :])

    def fits(m, lo, hi, row, end):
        return m + 1 < N and pitch_of(m + 1) == pitch_of(m) and row == lo and end == hi

    lift(1, 0, splits[1] + 1)
    done = splits[1] + 1
    pending = None
    for m in range(1, N):
        lo, hi, b = m, 32 - m, min(splits[m], 32 - m)
        need = b + 1
        if done < need:
            if pending:
                finish_from(*pending, low_ref)
                pending = None
            lift(m, done, need)
            done = need
        store_conv(m, lo, b, top_ref)
        if pending and fits(*pending, done, hi + 1):
            finish_lift(*pending, low_ref)
        else:
            if pending:
                finish_from(*pending, low_ref)
            lift(m, done, hi + 1)
        pending = (m, b, hi)
        early = m if m + 1 == N else max(m, min(b, splits[m + 1] + 1))
        store_conv(m, b, hi, low_ref)
        if b > lo and fits(m, lo, b, m, early):
            finish_lift(m, lo, b, top_ref)
        else:
            finish_from(m, lo, b, top_ref)
            if m + 1 < N:
                lift(m + 1, m, early)
        done = early
    finish_from(*pending, low_ref)
    g = jnp.concatenate([s_ref[15 * W1 + 16:15 * W1 + 32, :], s_ref[16 * W1 + 16:16 * W1 + 32, :]], axis=0)
    gt = g.T
    for n in range(N):
        for f in range(3):
            out_ref[n, :, 32 * f:32 * f + 32] = gt[4 * n + f:4 * n + f + 1, :]
        out_ref[n, :, 96:128] = jnp.zeros((1, 32), f32)

SPLITS = (0, 19, 18, 17, 16, 15, 14, 13, 17, 16, 15, 14, 20, 19, 18, 17)

def chain(recv, wt, lw, ow, cb, SPLITS=SPLITS, PIECE=384, ROLL=False):
    L = ROWS * W1
    vm = pl.BlockSpec(memory_space=pltpu.VMEM)
    return pl.pallas_call(
        functools.partial(chain_kernel, tuple(SPLITS), PIECE, ROLL),
        out_shape=jax.ShapeDtypeStruct((N, 1, 128), f32),
        in_specs=[vm] * 5, out_specs=vm,
        scratch_shapes=[pltpu.VMEM((64, 3 * L // 4), f32), pltpu.VMEM((L, 128), f32), pltpu.VMEM((L, 256), f32), pltpu.VMEM((L, 256), f32), pltpu.VMEM((L + 16 * 16, 256), f32),
                        pltpu.VMEM((L, 768), bf16), pltpu.VMEM((L, 768), bf16)],
        compiler_params=pltpu.CompilerParams(vmem_limit_bytes=48 * 2**20),
    )(recv, wt, lw, ow, cb)

def table_kernel(cw_ref, small_ref, wt_ref, lw_ref, owr_ref, rows_ref):
    for i in range(3):
        for j in range(3):
            wt_ref[i, 256 * j:256 * j + 256, :] = (0.5 * cw_ref[i, j].astype(f32)).T.astype(bf16)
    rows_ref[...] = jnp.zeros(rows_ref.shape, f32)
    w = small_ref[0:3, :]
    hi = w.astype(bf16).astype(f32)
    rows_ref[0:3, :] = hi
    rows_ref[8:11, :] = w - hi
    b = small_ref[3:4, :]
    bhi = b.astype(bf16).astype(f32)
    rows_ref[3:4, :] = bhi
    rows_ref[11:12, :] = b - bhi
    k = lax.broadcasted_iota(jnp.int32, (256, 16), 0)
    col = lax.broadcasted_iota(jnp.int32, (256, 16), 1)
    field = k & 3
    weight = (k < 192) & (field < 3) & (col == field + jnp.where(k < 128, 0, 8))
    bias = ((k == 192) & (col == 3)) | ((k == 193) & (col == 11))
    pick = jnp.where(weight | bias, 1.0, 0.0).astype(bf16)
    lw_ref[...] = jnp.dot(pick, rows_ref[...].astype(bf16), preferred_element_type=f32).astype(bf16)
    rows_ref[...] = jnp.zeros(rows_ref.shape, f32)
    rows_ref[0:3, :] = 0.5 * small_ref[4:7, :]
    lane = lax.broadcasted_iota(jnp.int32, (128, 16), 0) & 3
    pick = jnp.where((lane < 3) & (lane == lax.broadcasted_iota(jnp.int32, (128, 16), 1)), 1.0, 0.0).astype(bf16)
    owr_ref[...] = jnp.dot(pick, rows_ref[...].astype(bf16), preferred_element_type=f32).T.astype(bf16)

def tables(lift_weight, lift_bias, conv_weight, conv_bias, out_weight):
    vm = pl.BlockSpec(memory_space=pltpu.VMEM)
    wt, lw, ow = pl.pallas_call(
        table_kernel,
        out_shape=[jax.ShapeDtypeStruct((3, 768, 256), bf16), jax.ShapeDtypeStruct((256, 256), bf16), jax.ShapeDtypeStruct((256, 128), bf16)],
        in_specs=[vm] * 2, out_specs=[vm] * 3,
        scratch_shapes=[pltpu.VMEM((16, 256), f32)],
        compiler_params=pltpu.CompilerParams(vmem_limit_bytes=32 * 2**20),
        cost_estimate=pl.CostEstimate(flops=10**7, bytes_accessed=10**7, transcendentals=0), name="tables",
    )(conv_weight, jnp.concatenate([lift_weight.T, lift_bias[None], out_weight.astype(f32)], axis=0))
    return wt, lw, ow, conv_bias[None]

def thirds(x):
    hi = x.astype(bf16)
    rest = x - hi.astype(f32)
    mid = rest.astype(bf16)
    low = (rest - mid.astype(f32)).astype(bf16)
    return jnp.concatenate([hi, mid, low], axis=0)

def exact_dot(x, pattern):
    n = x.shape[0]
    y = jnp.dot(thirds(x), pattern, preferred_element_type=f32)
    return y[0:n] + y[n:2 * n] + y[2 * n:3 * n]

def fine_step(a, b, q):
    def parts(x):
        e, w = pltpu.roll(x, x.shape[1] - 1, 1), pltpu.roll(x, 1, 1)
        n, s = pltpu.roll(x, 1, 0), pltpu.roll(x, x.shape[0] - 1, 0)
        return e - w, s - n, (e + w) + (n + s)
    ax, ay, al = parts(a)
    bx, by, bl = parts(b)
    qx, qy, ql = parts(q)
    half, keep = 0.5 * time_step, 1.0 - 4.0 * time_step * viscosity
    new_a = keep * a + time_step * viscosity * al - half * (a * ax + b * ay + qx)
    new_b = keep * b + time_step * viscosity * bl - half * (a * bx + b * by + qy)
    new_q = keep * q + time_step * viscosity * ql - half * sound_sq * (ax + by)
    return new_a, new_b, new_q

def edge_kernel(s_ref, up_ref, down_ref):
    up_ref[3, 3:4, :] = jnp.zeros((1, s_ref.shape[3]), f32)
    down_ref[3, 3:4, :] = jnp.zeros((1, s_ref.shape[3]), f32)
    for f in range(3):
        up_ref[f] = s_ref[0, f, 12:16, :]
        up_ref[3, f:f + 1, :] = jnp.sum(s_ref[0, f, 8:16, :], axis=0, keepdims=True)
        down_ref[f] = s_ref[0, f, 0:4, :]
        down_ref[3, f:f + 1, :] = jnp.sum(s_ref[0, f, 0:8, :], axis=0, keepdims=True)

def first_kernel(tm_ref, s_ref, up_ref, dn_ref, wt_ref, lw_ref, ow_ref, cb_ref, fine_ref, delta_ref, c_ref, q_ref, qf_ref, h_ref):
    blank = jnp.zeros((4, s_ref.shape[3]), f32)
    fields = [jnp.concatenate([blank, up_ref[f], s_ref[0, f], dn_ref[f], blank], axis=0) for f in range(3)]
    q_ref[...] = jnp.zeros(q_ref.shape, f32)
    qf_ref[...] = jnp.zeros(qf_ref.shape, f32)
    q_ref[0:4, :] = up_ref[3]
    q_ref[12:16, :] = dn_ref[3]
    for f in range(3):
        for r in range(2):
            q_ref[4 + 4 * r + f:5 + 4 * r + f, :] = jnp.sum(s_ref[0, f, 8 * r:8 * r + 8, :], axis=0, keepdims=True)
    half = 128 * RF
    pool = (lax.broadcasted_iota(jnp.int32, (half, 128), 0) // RF == lax.broadcasted_iota(jnp.int32, (half, 128), 1)).astype(f32).astype(bf16)

    def pooled(ref):
        return jnp.concatenate([exact_dot(ref[:, 0:half], pool), exact_dot(ref[:, half:], pool)], axis=1) * (1.0 / (RF * RF))
    start = pooled(q_ref)
    pad = jnp.zeros((48, 256), f32)
    s = jnp.concatenate([start, pad, start, pad], axis=0).T
    x = lift_operand(s, lax.broadcasted_iota(jnp.int32, s.shape, 1))
    krow = lax.broadcasted_iota(jnp.int32, (256, 256), 0)
    kslot = (krow & 63) >> 2
    lw = lw_ref[...].astype(f32)
    fields = fine_step(*fields)
    for r in range(4):
        lwm = jnp.where((kslot == r) | (krow >= 192), lw, 0.0).astype(bf16)
        h = twice_gelu(jnp.dot(x, lwm, preferred_element_type=f32))
        left, right = shifted(h, 256)
        h_ref[256 * r:256 * r + 256, 0:256] = left.astype(bf16)
        h_ref[256 * r:256 * r + 256, 256:512] = h.astype(bf16)
        h_ref[256 * r:256 * r + 256, 512:768] = right.astype(bf16)
    fields = fine_step(*fields)
    acc = jnp.dot(h_ref[0:512], wt_ref[0], preferred_element_type=f32)
    acc = acc + jnp.dot(h_ref[256:768], wt_ref[1], preferred_element_type=f32)
    acc = acc + jnp.dot(h_ref[512:1024], wt_ref[2], preferred_element_type=f32)
    fields = fine_step(*fields)
    act = twice_gelu(acc + cb_ref[...]).astype(bf16)
    inc = jnp.dot(act, ow_ref[...], preferred_element_type=f32)
    lane = lax.broadcasted_iota(jnp.int32, s.shape, 1)
    guess = (s + jnp.where(lane < 8, inc[0:256], inc[256:512])).T[4:12]
    for _ in range(FINE - 3):
        fields = fine_step(*fields)
    for f in range(3):
        for r in range(2):
            qf_ref[4 * r + f:4 * r + f + 1, :] = jnp.sum(fields[f][8 + 8 * r:16 + 8 * r], axis=0, keepdims=True)
    first = jnp.where(tm_ref[0] == 0, guess, 0.0)
    c = first + (pooled(qf_ref) - guess)
    for i in range(c_ref.shape[0]):
        c_ref[i] = c
    delta_ref[...] = guess - first
    for f in range(3):
        fine_ref[f] = fields[f][8:24]

def subtract_kernel(fine_ref, delta_ref, corr_ref):
    half = 128 * RF
    spread = (lax.broadcasted_iota(jnp.int32, (128, half), 1) // RF == lax.broadcasted_iota(jnp.int32, (128, half), 0)).astype(f32).astype(bf16)
    for p in range(2):
        wide = exact_dot(delta_ref[:, 128 * p:128 * p + 128], spread)
        for f in range(3):
            for r in range(2):
                at = pl.ds(half * p, half)
                corr_ref[f, 8 * r:8 * r + 8, at] = fine_ref[f, 8 * r:8 * r + 8, at] - wide[4 * r + f:4 * r + f + 1]

def window_kernel(sp_ref, b_ref, out_ref, w_ref):
    count = b_ref.shape[0]
    for q in range(ROWS):
        dev = lax.rem(sp_ref[0] + (count - 8 + (q + 1) // 2), count)
        r = (q + 1) % 2
        for f in range(3):
            w_ref[3 * (q % 8) + f, q // 8:q // 8 + 1, :] = b_ref[dev, 4 * r + f:4 * r + f + 1, :]
    for i in range(8):
        for f in range(3):
            v = w_ref[3 * i + f]
            ext = jnp.concatenate([v[:, 240:256], v, v[:, 0:16]], axis=1)
            at = f * 8 * W1 + i * W1
            for j in range(N):
                out_ref[j, :, at:at + W1] = ext[:, 16 * j:16 * j + W1]

def last_kernel(g_ref, corr_ref, out_ref, y_ref):
    for j in range(N):
        y_ref[j:j + 1, :] = g_ref[j]
    parts = thirds(y_ref[...])
    row = lax.broadcasted_iota(jnp.int32, (128, 128), 0)
    col = lax.broadcasted_iota(jnp.int32, (128, 128), 1)
    for r in range(2):
        for f in range(3):
            pattern = (row - 32 * f - 16 * r == col // RF).astype(f32).astype(bf16)
            y = jnp.dot(parts, pattern, preferred_element_type=f32)
            y = y[0:N] + y[N:2 * N] + y[2 * N:3 * N]
            for j in range(N):
                at = 128 * j
                out_ref[0, f, 8 * r:8 * r + 8, at:at + 128] = corr_ref[f, 8 * r:8 * r + 8, at:at + 128] + y[j:j + 1]

def shards(start_states, lift_weight, lift_bias, conv_weight, conv_bias, out_weight):
    vm = pl.BlockSpec(memory_space=pltpu.VMEM)
    sm = pl.BlockSpec(memory_space=pltpu.SMEM)
    params = pltpu.CompilerParams(vmem_limit_bytes=48 * 2**20)
    count = lax.axis_size("space")
    slab = start_states[0]
    edges = jax.ShapeDtypeStruct((4, 4, slab.shape[2]), f32)
    up, down = pl.pallas_call(edge_kernel, out_shape=[edges, edges], in_specs=[vm], out_specs=[vm, vm], compiler_params=params, name="edges")(start_states)
    up = lax.ppermute(up, "space", [(i, (i + 1) % count) for i in range(count)])
    down = lax.ppermute(down, "space", [((i + 1) % count, i) for i in range(count)])
    weights = tables(lift_weight, lift_bias, conv_weight, conv_bias, out_weight)
    tm = lax.axis_index("tm").astype(jnp.int32).reshape(1)
    sp = lax.axis_index("space").astype(jnp.int32).reshape(1)
    fine, delta, c = pl.pallas_call(
        first_kernel,
        out_shape=[jax.ShapeDtypeStruct(slab.shape, f32), jax.ShapeDtypeStruct((8, 256), f32), jax.ShapeDtypeStruct((count, 8, 256), f32)],
        in_specs=[sm] + [vm] * 7, out_specs=[vm] * 3,
        scratch_shapes=[pltpu.VMEM((16, slab.shape[2]), f32), pltpu.VMEM((8, slab.shape[2]), f32), pltpu.VMEM((1024, 768), bf16)],
        compiler_params=params, name="fine_and_guess",
    )(tm, start_states, up, down, *weights)
    c = lax.all_to_all(c, "space", 0, 0)
    corr = pl.pallas_call(
        subtract_kernel, out_shape=jax.ShapeDtypeStruct(slab.shape, f32), in_specs=[vm, vm], out_specs=vm, compiler_params=params,
        cost_estimate=pl.CostEstimate(flops=10**6, bytes_accessed=10**6, transcendentals=0), name="subtract",
    )(fine, delta)
    send = pl.pallas_call(
        window_kernel, out_shape=jax.ShapeDtypeStruct((N, 4, 3 * ROWS * W1 // 4), f32),
        in_specs=[sm, vm], out_specs=vm, scratch_shapes=[pltpu.VMEM((24, 4, 256), f32)],
        compiler_params=params, name="windows",
    )(sp, c)
    recv = lax.all_to_all(send, "tm", 0, 0)
    g = chain(recv, *weights)
    g = lax.all_to_all(g, "tm", 0, 0)
    return pl.pallas_call(
        last_kernel, out_shape=jax.ShapeDtypeStruct(start_states.shape, f32),
        in_specs=[vm, vm], out_specs=vm, scratch_shapes=[pltpu.VMEM((N, 128), f32)],
        compiler_params=params, name="correct",
    )(g, corr)

def solution(mesh):
    return jax.shard_map(
        shards, mesh=mesh,
        in_specs=(P("tm", None, "space", None), P(), P(), P(), P(), P()),
        out_specs=P("tm", None, "space", None), check_vma=False,
    )
```

```python
import functools
import jax, jax.numpy as jnp
from jax import lax
from jax.experimental import pallas as pl
from jax.experimental.pallas import tpu as pltpu
from jax.sharding import PartitionSpec as P

f32, bf16 = jnp.float32, jnp.bfloat16
FINE = 4
RF = 8
time_step = 0.2
viscosity = 1.0
sound_sq = 1.0
N = 16
ROWS = 32
W1, W2 = 48, 32

def twice_gelu(x):
    u = x * (0.7978845608028654 + 0.035677408136300125 * (x * x))
    return x + x * jnp.tanh(u)

def lift_operand(s, lane):
    hi = s.astype(bf16)
    lo = (s - hi.astype(f32)).astype(bf16)
    one = jnp.ones_like(hi)
    return jnp.concatenate([jnp.where(lane < 64, hi, lo), jnp.where(lane < 64, hi, one)], axis=1)

def shifted(h, axis_size):
    return pltpu.roll(h, 1, 0), pltpu.roll(h, axis_size - 1, 0)

def chain_kernel(SPLITS, PIECE, ROLL, r_ref, wt_ref, lw_ref, ow_ref, cb_ref, out_ref, d_ref, s_ref, top_ref, low_ref, y_ref, *h_refs):
    part = ROWS * W1 // 4
    acc = r_ref[0]
    d_ref[0:4] = jnp.zeros((4, 3 * part), f32)
    d_ref[4:8] = acc
    for n in range(1, N - 1):
        acc = acc + r_ref[n]
        d_ref[4 * n + 4:4 * n + 8] = acc
    field = lax.broadcasted_iota(jnp.int32, (128, 128), 1) & 3
    for t in range(part // 128):
        turned = [d_ref[:, f * part + t * 128:f * part + t * 128 + 128].T for f in range(3)]
        turned = [jnp.concatenate([x, x], axis=1) for x in turned]
        for u in range(4):
            s = jnp.zeros((128, 128), f32)
            for f in range(3):
                moved = turned[f] if f == u else pltpu.roll(turned[f], (f - u) % 128, 1)
                s = jnp.where(field == f, moved, s)
            s_ref[u * part + t * 128:u * part + t * 128 + 128, :] = s
    krow = lax.broadcasted_iota(jnp.int32, (256, 256), 0)
    kslot = (krow & 63) >> 2
    ocol = (lax.broadcasted_iota(jnp.int32, (256, 128), 1) & 63) >> 2
    lw, ow = lw_ref[...].astype(f32), ow_ref[...].astype(f32)

    def rows_of(row, n, pitch):
        if pitch == W1:
            return [pl.ds(row * W1, n * W1)]
        return [pl.ds((row + i) * W1 + (W1 - pitch) // 2, pitch) for i in range(n)]

    def pitch_of(m):
        return W1 if m < 8 else W2

    def lift(m, lo, hi):
        if hi <= lo:
            return
        n, pitch, h = hi - lo, pitch_of(m), h_refs[m % 2]
        cells = n * pitch
        s = jnp.concatenate([s_ref[d, :] for d in rows_of(lo, n, pitch)], axis=0)
        lane = lax.broadcasted_iota(jnp.int32, s.shape, 1)
        lwm = jnp.where((kslot == m) | (krow >= 192), lw, 0.0).astype(bf16)
        y = twice_gelu(jnp.dot(lift_operand(s, lane), lwm, preferred_element_type=f32))
        y_ref[8:8 + cells, :] = y
        left, right = y_ref[7:7 + cells, :], y_ref[9:9 + cells, :]
        dst = pl.ds(lo * pitch, cells)
        h[dst, 0:256] = left.astype(bf16)
        h[dst, 256:512] = y.astype(bf16)
        h[dst, 512:768] = right.astype(bf16)

    def conv(m, lo, hi):
        n, pitch, h = hi - lo, pitch_of(m), h_refs[m % 2]
        x = jnp.concatenate([h[pl.ds((lo + di - 1) * pitch, n * pitch), :] for di in range(3)], axis=1)
        return jnp.dot(x, wt_ref[...].reshape(2304, 256), preferred_element_type=f32)

    def finish(m, lo, hi, acc):
        n, pitch = hi - lo, pitch_of(m)
        act = twice_gelu(acc + cb_ref[...]).astype(bf16)
        owm = jnp.where(ocol >= m, ow, 0.0).astype(bf16)
        inc = jnp.dot(act, owm, preferred_element_type=f32)
        at = 0
        for d in rows_of(lo, n, pitch):
            s_ref[d, :] = s_ref[d, :] + inc[at:at + d.size]
            at += d.size

    def finish_lift(m, lo, hi, acc_ref):
        pitch, h = pitch_of(m), h_refs[(m + 1) % 2]
        lwm = jnp.where((kslot == m + 1) | (krow >= 192), lw, 0.0).astype(bf16)
        owm = jnp.where(ocol >= m, ow, 0.0).astype(bf16)
        count = max(1, round((hi - lo) * pitch / PIECE))
        cuts = [lo + (hi - lo) * i // count for i in range(count + 1)]
        for p, (at, end) in enumerate(zip(cuts[:-1], cuts[1:])):
            if end <= at:
                continue
            cells, base = (end - at) * pitch, (at - lo) * pitch
            act = twice_gelu(acc_ref[base:base + cells, :] + cb_ref[...]).astype(bf16)
            inc = jnp.dot(act, owm, preferred_element_type=f32)
            news, off = [], 0
            for d in rows_of(at, end - at, pitch):
                new = s_ref[d, :] + inc[off:off + d.size]
                s_ref[d, :] = new
                news.append(new)
                off += d.size
            s = jnp.concatenate(news, axis=0)
            lane = lax.broadcasted_iota(jnp.int32, s.shape, 1)
            y = twice_gelu(jnp.dot(lift_operand(s, lane), lwm, preferred_element_type=f32))
            dst = pl.ds(at * pitch, cells)
            if ROLL:
                left, right = shifted(y, cells)
            else:
                top = 8 + at * pitch + 16 * p
                y_ref[top:top + cells, :] = y
                left, right = y_ref[top - 1:top - 1 + cells, :], y_ref[top + 1:top + 1 + cells, :]
            h[dst, 0:256] = left.astype(bf16)
            h[dst, 256:512] = y.astype(bf16)
            h[dst, 512:768] = right.astype(bf16)

    splits = SPLITS

    def block(body):
        body()

    def store_conv(m, lo, hi, acc_ref):
        if hi > lo:
            acc_ref[0:(hi - lo) * pitch_of(m), :] = conv(m, lo, hi)

    def finish_from(m, lo, hi, acc_ref):
        if hi > lo:
            finish(m, lo, hi, acc_ref[0:(hi - lo) * pitch_of(m), :])

    def fits(m, lo, hi, row, end):
        return m + 1 < N and pitch_of(m + 1) == pitch_of(m) and row == lo and end == hi

    lift(1, 0, splits[1] + 1)
    done = splits[1] + 1
    pending = None
    for m in range(1, N):
        lo, hi, b = m, 32 - m, min(splits[m], 32 - m)
        need = b + 1
        if done < need:
            if pending:
                finish_from(*pending, low_ref)
                pending = None
            lift(m, done, need)
            done = need
        store_conv(m, lo, b, top_ref)
        if pending and fits(*pending, done, hi + 1):
            finish_lift(*pending, low_ref)
        else:
            if pending:
                finish_from(*pending, low_ref)
            lift(m, done, hi + 1)
        pending = (m, b, hi)
        early = m if m + 1 == N else max(m, min(b, splits[m + 1] + 1))
        store_conv(m, b, hi, low_ref)
        if b > lo and fits(m, lo, b, m, early):
            finish_lift(m, lo, b, top_ref)
        else:
            finish_from(m, lo, b, top_ref)
            if m + 1 < N:
                lift(m + 1, m, early)
        done = early
    finish_from(*pending, low_ref)
    g = jnp.concatenate([s_ref[15 * W1 + 16:15 * W1 + 32, :], s_ref[16 * W1 + 16:16 * W1 + 32, :]], axis=0)
    gt = g.T
    for n in range(N):
        for f in range(3):
            out_ref[n, :, 32 * f:32 * f + 32] = gt[4 * n + f:4 * n + f + 1, :]
        out_ref[n, :, 96:128] = jnp.zeros((1, 32), f32)

SPLITS = (0, 18, 17, 16, 15, 14, 13, 12, 18, 17, 16, 15, 20, 19, 18, 17)

def chain(recv, wt, lw, ow, cb, SPLITS=SPLITS, PIECE=384, ROLL=False):
    L = ROWS * W1
    vm = pl.BlockSpec(memory_space=pltpu.VMEM)
    return pl.pallas_call(
        functools.partial(chain_kernel, tuple(SPLITS), PIECE, ROLL),
        out_shape=jax.ShapeDtypeStruct((N, 1, 128), f32),
        in_specs=[vm] * 5, out_specs=vm,
        scratch_shapes=[pltpu.VMEM((64, 3 * L // 4), f32), pltpu.VMEM((L, 128), f32), pltpu.VMEM((L, 256), f32), pltpu.VMEM((L, 256), f32), pltpu.VMEM((L + 16 * 16, 256), f32),
                        pltpu.VMEM((L, 768), bf16), pltpu.VMEM((L, 768), bf16)],
        compiler_params=pltpu.CompilerParams(vmem_limit_bytes=48 * 2**20),
    )(recv, wt, lw, ow, cb)

def table_kernel(cw_ref, small_ref, wt_ref, lw_ref, owr_ref, rows_ref):
    for i in range(3):
        for j in range(3):
            wt_ref[i, 256 * j:256 * j + 256, :] = (0.5 * cw_ref[i, j].astype(f32)).T.astype(bf16)
    rows_ref[...] = jnp.zeros(rows_ref.shape, f32)
    w = small_ref[0:3, :]
    hi = w.astype(bf16).astype(f32)
    rows_ref[0:3, :] = hi
    rows_ref[8:11, :] = w - hi
    b = small_ref[3:4, :]
    bhi = b.astype(bf16).astype(f32)
    rows_ref[3:4, :] = bhi
    rows_ref[11:12, :] = b - bhi
    k = lax.broadcasted_iota(jnp.int32, (256, 16), 0)
    col = lax.broadcasted_iota(jnp.int32, (256, 16), 1)
    field = k & 3
    weight = (k < 192) & (field < 3) & (col == field + jnp.where(k < 128, 0, 8))
    bias = ((k == 192) & (col == 3)) | ((k == 193) & (col == 11))
    pick = jnp.where(weight | bias, 1.0, 0.0).astype(bf16)
    lw_ref[...] = jnp.dot(pick, rows_ref[...].astype(bf16), preferred_element_type=f32).astype(bf16)
    rows_ref[...] = jnp.zeros(rows_ref.shape, f32)
    rows_ref[0:3, :] = 0.5 * small_ref[4:7, :]
    lane = lax.broadcasted_iota(jnp.int32, (128, 16), 0) & 3
    pick = jnp.where((lane < 3) & (lane == lax.broadcasted_iota(jnp.int32, (128, 16), 1)), 1.0, 0.0).astype(bf16)
    owr_ref[...] = jnp.dot(pick, rows_ref[...].astype(bf16), preferred_element_type=f32).T.astype(bf16)

def tables(lift_weight, lift_bias, conv_weight, conv_bias, out_weight):
    vm = pl.BlockSpec(memory_space=pltpu.VMEM)
    wt, lw, ow = pl.pallas_call(
        table_kernel,
        out_shape=[jax.ShapeDtypeStruct((3, 768, 256), bf16), jax.ShapeDtypeStruct((256, 256), bf16), jax.ShapeDtypeStruct((256, 128), bf16)],
        in_specs=[vm] * 2, out_specs=[vm] * 3,
        scratch_shapes=[pltpu.VMEM((16, 256), f32)],
        compiler_params=pltpu.CompilerParams(vmem_limit_bytes=32 * 2**20),
        cost_estimate=pl.CostEstimate(flops=10**7, bytes_accessed=10**7, transcendentals=0), name="tables",
    )(conv_weight, jnp.concatenate([lift_weight.T, lift_bias[None], out_weight.astype(f32)], axis=0))
    return wt, lw, ow, conv_bias[None]

def thirds(x):
    hi = x.astype(bf16)
    rest = x - hi.astype(f32)
    mid = rest.astype(bf16)
    low = (rest - mid.astype(f32)).astype(bf16)
    return jnp.concatenate([hi, mid, low], axis=0)

def exact_dot(x, pattern):
    n = x.shape[0]
    y = jnp.dot(thirds(x), pattern, preferred_element_type=f32)
    return y[0:n] + y[n:2 * n] + y[2 * n:3 * n]

def fine_step(a, b, q):
    def parts(x):
        e, w = pltpu.roll(x, x.shape[1] - 1, 1), pltpu.roll(x, 1, 1)
        n, s = pltpu.roll(x, 1, 0), pltpu.roll(x, x.shape[0] - 1, 0)
        return e - w, s - n, (e + w) + (n + s)
    ax, ay, al = parts(a)
    bx, by, bl = parts(b)
    qx, qy, ql = parts(q)
    half, keep = 0.5 * time_step, 1.0 - 4.0 * time_step * viscosity
    new_a = keep * a + time_step * viscosity * al - half * (a * ax + b * ay + qx)
    new_b = keep * b + time_step * viscosity * bl - half * (a * bx + b * by + qy)
    new_q = keep * q + time_step * viscosity * ql - half * sound_sq * (ax + by)
    return new_a, new_b, new_q

def edge_kernel(s_ref, up_ref, down_ref):
    up_ref[3, 3:4, :] = jnp.zeros((1, s_ref.shape[3]), f32)
    down_ref[3, 3:4, :] = jnp.zeros((1, s_ref.shape[3]), f32)
    for f in range(3):
        up_ref[f] = s_ref[0, f, 12:16, :]
        up_ref[3, f:f + 1, :] = jnp.sum(s_ref[0, f, 8:16, :], axis=0, keepdims=True)
        down_ref[f] = s_ref[0, f, 0:4, :]
        down_ref[3, f:f + 1, :] = jnp.sum(s_ref[0, f, 0:8, :], axis=0, keepdims=True)

def first_kernel(tm_ref, s_ref, up_ref, dn_ref, wt_ref, lw_ref, ow_ref, cb_ref, corr_ref, c_ref, q_ref, qf_ref, h_ref):
    blank = jnp.zeros((4, s_ref.shape[3]), f32)
    fields = [jnp.concatenate([blank, up_ref[f], s_ref[0, f], dn_ref[f], blank], axis=0) for f in range(3)]
    q_ref[...] = jnp.zeros(q_ref.shape, f32)
    qf_ref[...] = jnp.zeros(qf_ref.shape, f32)
    q_ref[0:4, :] = up_ref[3]
    q_ref[12:16, :] = dn_ref[3]
    for f in range(3):
        for r in range(2):
            q_ref[4 + 4 * r + f:5 + 4 * r + f, :] = jnp.sum(s_ref[0, f, 8 * r:8 * r + 8, :], axis=0, keepdims=True)
    half = 128 * RF
    pool = (lax.broadcasted_iota(jnp.int32, (half, 128), 0) // RF == lax.broadcasted_iota(jnp.int32, (half, 128), 1)).astype(f32).astype(bf16)
    spread = (lax.broadcasted_iota(jnp.int32, (128, half), 1) // RF == lax.broadcasted_iota(jnp.int32, (128, half), 0)).astype(f32).astype(bf16)

    def pooled(ref):
        return jnp.concatenate([exact_dot(ref[:, 0:half], pool), exact_dot(ref[:, half:], pool)], axis=1) * (1.0 / (RF * RF))
    start = pooled(q_ref)
    pad = jnp.zeros((48, 256), f32)
    s = jnp.concatenate([start, pad, start, pad], axis=0).T
    x = lift_operand(s, lax.broadcasted_iota(jnp.int32, s.shape, 1))
    krow = lax.broadcasted_iota(jnp.int32, (256, 256), 0)
    kslot = (krow & 63) >> 2
    lw = lw_ref[...].astype(f32)
    fields = fine_step(*fields)
    for r in range(4):
        lwm = jnp.where((kslot == r) | (krow >= 192), lw, 0.0).astype(bf16)
        h = twice_gelu(jnp.dot(x, lwm, preferred_element_type=f32))
        left, right = shifted(h, 256)
        h_ref[256 * r:256 * r + 256, 0:256] = left.astype(bf16)
        h_ref[256 * r:256 * r + 256, 256:512] = h.astype(bf16)
        h_ref[256 * r:256 * r + 256, 512:768] = right.astype(bf16)
    fields = fine_step(*fields)
    acc = jnp.dot(h_ref[0:512], wt_ref[0], preferred_element_type=f32)
    acc = acc + jnp.dot(h_ref[256:768], wt_ref[1], preferred_element_type=f32)
    acc = acc + jnp.dot(h_ref[512:1024], wt_ref[2], preferred_element_type=f32)
    fields = fine_step(*fields)
    act = twice_gelu(acc + cb_ref[...]).astype(bf16)
    inc = jnp.dot(act, ow_ref[...], preferred_element_type=f32)
    lane = lax.broadcasted_iota(jnp.int32, s.shape, 1)
    guess = (s + jnp.where(lane < 8, inc[0:256], inc[256:512])).T[4:12]
    for _ in range(FINE - 3):
        fields = fine_step(*fields)
    for f in range(3):
        for r in range(2):
            qf_ref[4 * r + f:4 * r + f + 1, :] = jnp.sum(fields[f][8 + 8 * r:16 + 8 * r], axis=0, keepdims=True)
    first = jnp.where(tm_ref[0] == 0, guess, 0.0)
    c = first + (pooled(qf_ref) - guess)
    for i in range(c_ref.shape[0]):
        c_ref[i] = c
    delta = guess - first
    for p in range(2):
        wide = exact_dot(delta[:, 128 * p:128 * p + 128], spread)
        for f in range(3):
            for r in range(2):
                corr_ref[f, 8 * r:8 * r + 8, half * p:half * p + half] = fields[f][8 + 8 * r:16 + 8 * r, half * p:half * p + half] - wide[4 * r + f:4 * r + f + 1]

def window_kernel(sp_ref, b_ref, out_ref, w_ref):
    count = b_ref.shape[0]
    for q in range(ROWS):
        dev = lax.rem(sp_ref[0] + (count - 8 + (q + 1) // 2), count)
        r = (q + 1) % 2
        for f in range(3):
            w_ref[3 * (q % 8) + f, q // 8:q // 8 + 1, :] = b_ref[dev, 4 * r + f:4 * r + f + 1, :]
    for i in range(8):
        for f in range(3):
            v = w_ref[3 * i + f]
            ext = jnp.concatenate([v[:, 240:256], v, v[:, 0:16]], axis=1)
            at = f * 8 * W1 + i * W1
            for j in range(N):
                out_ref[j, :, at:at + W1] = ext[:, 16 * j:16 * j + W1]

def last_kernel(g_ref, corr_ref, out_ref, y_ref):
    for j in range(N):
        y_ref[j:j + 1, :] = g_ref[j]
    parts = thirds(y_ref[...])
    row = lax.broadcasted_iota(jnp.int32, (128, 128), 0)
    col = lax.broadcasted_iota(jnp.int32, (128, 128), 1)
    for r in range(2):
        for f in range(3):
            pattern = (row - 32 * f - 16 * r == col // RF).astype(f32).astype(bf16)
            y = jnp.dot(parts, pattern, preferred_element_type=f32)
            y = y[0:N] + y[N:2 * N] + y[2 * N:3 * N]
            for j in range(N):
                at = 128 * j
                out_ref[0, f, 8 * r:8 * r + 8, at:at + 128] = corr_ref[f, 8 * r:8 * r + 8, at:at + 128] + y[j:j + 1]

def shards(start_states, lift_weight, lift_bias, conv_weight, conv_bias, out_weight):
    vm = pl.BlockSpec(memory_space=pltpu.VMEM)
    sm = pl.BlockSpec(memory_space=pltpu.SMEM)
    params = pltpu.CompilerParams(vmem_limit_bytes=48 * 2**20)
    count = lax.axis_size("space")
    slab = start_states[0]
    edges = jax.ShapeDtypeStruct((4, 4, slab.shape[2]), f32)
    up, down = pl.pallas_call(edge_kernel, out_shape=[edges, edges], in_specs=[vm], out_specs=[vm, vm], compiler_params=params, name="edges")(start_states)
    up = lax.ppermute(up, "space", [(i, (i + 1) % count) for i in range(count)])
    down = lax.ppermute(down, "space", [((i + 1) % count, i) for i in range(count)])
    weights = tables(lift_weight, lift_bias, conv_weight, conv_bias, out_weight)
    tm = lax.axis_index("tm").astype(jnp.int32).reshape(1)
    sp = lax.axis_index("space").astype(jnp.int32).reshape(1)
    corr, c = pl.pallas_call(
        first_kernel,
        out_shape=[jax.ShapeDtypeStruct(slab.shape, f32), jax.ShapeDtypeStruct((count, 8, 256), f32)],
        in_specs=[sm] + [vm] * 7, out_specs=[vm, vm],
        scratch_shapes=[pltpu.VMEM((16, slab.shape[2]), f32), pltpu.VMEM((8, slab.shape[2]), f32), pltpu.VMEM((1024, 768), bf16)],
        compiler_params=params, name="fine_and_guess",
    )(tm, start_states, up, down, *weights)
    c = lax.all_to_all(c, "space", 0, 0)
    send = pl.pallas_call(
        window_kernel, out_shape=jax.ShapeDtypeStruct((N, 4, 3 * ROWS * W1 // 4), f32),
        in_specs=[sm, vm], out_specs=vm, scratch_shapes=[pltpu.VMEM((24, 4, 256), f32)],
        compiler_params=params, name="windows",
    )(sp, c)
    recv = lax.all_to_all(send, "tm", 0, 0)
    g = chain(recv, *weights)
    g = lax.all_to_all(g, "tm", 0, 0)
    return pl.pallas_call(
        last_kernel, out_shape=jax.ShapeDtypeStruct(start_states.shape, f32),
        in_specs=[vm, vm], out_specs=vm, scratch_shapes=[pltpu.VMEM((N, 128), f32)],
        compiler_params=params, name="correct",
    )(g, corr)

def solution(mesh):
    return jax.shard_map(
        shards, mesh=mesh,
        in_specs=(P("tm", None, "space", None), P(), P(), P(), P(), P()),
        out_specs=P("tm", None, "space", None), check_vma=False,
    )
```
